256 devices in a mesh: seq: 32 (over y_hi, z, core), mp: 2 (over y_lo), batch: 4 (over x).
Axes of the slice: x: 4, y: 4 (y_hi: 2, y_lo: 2; y = y_hi * 2 + y_lo), z: 8, core: 2. Of those that a mesh axis runs over, the one named last changes fastest.
Arguments:
- conv_input: bfloat16 [4, 65536, 768], P('batch', 'seq'), may hold values from -6 to 6
- pre_activation: bfloat16 [4, 65536, 768], P('batch', 'seq', 'mp'), may hold values from -6 to 6
- track_gradient: bfloat16 [4, 65536, 768], P('batch', 'seq', 'mp'), may hold values from -6 to 6
- kernel: bfloat16 [5, 768, 768], P(None, None, 'mp'), may hold values from -0.09375 to 0.09375
- pair_rows: int32 [4, 16384, 2], P('batch', 'seq'), may hold values from 0 to 65535, as said below
- pair_count: int32 [4, 32], P('batch', 'seq'), may hold values from 256 to 512
- pair_gradient: bfloat16 [4, 16384, 2, 768], P('batch', 'seq', None, 'mp'), may hold values from -6 to 6
Outputs:
- grad_skip: bfloat16 [4, 65536, 768], P('batch', ('seq', 'mp'))
- grad_lower: bfloat16 [4, 32768, 768], P('batch', ('seq', 'mp'))
- grad_weight: float32 [5, 768, 768], P(None, 'seq', 'mp')
The draws below stay inside these ranges and needn't reach their ends.
Inputs may be any that keep to these rules, and one draw needn't show every extreme that they name: `pair_rows`: A window's pair slots stand in 32 blocks of 512, block s on index s of seq, and the rows of index t of seq are t * 2048 to (t + 1) * 2048 - 1. In every block at most 96 of the 1024 endpoints (padding slots included) lie in the rows of any one index of seq, and in every window one index of seq holds exactly 96 endpoints of every block. A pair's donor row is not above its acceptor row. The first pair_count slots of a block are real pairs; the others are padding whose gradients count for nothing.
All inputs are finite; a program needn't handle non-finite values.
Results may differ from the reference program's by a relative error of at most 0.0049.
Values may be sent and summed in bfloat16 or wider, within the bound.
A program may use at most 128 MiB of HBM per device.

```python
import math
import jax
import jax.numpy as jnp
from jax import lax

D = 768
KW = 5
ROWS_DEV = 2048
P_DEV = 512
WINDOWS = 4
LENGTH = 65536
PAIRS = 16384
CAP = 96
N_SEQ = 32


def draw_pair_rows(key, part):
    key = jax.random.fold_in(key, 7)
    slots_total = N_SEQ * CAP
    endpoints = 2 * P_DEV
    window_keys = jax.random.split(key, WINDOWS)

    def one_window(window_key):
        forced_key, block_key = jax.random.split(window_key)
        forced = jax.random.randint(forced_key, (), 0, N_SEQ)
        block_keys = jax.random.split(block_key, N_SEQ)

        def one_block(block_seed):
            jitter_key, order_key, offset_key = jax.random.split(block_seed, 3)
            slot_ids = jnp.arange(slots_total, dtype=jnp.int32)
            owners = slot_ids // CAP
            jitter_vals = jax.random.randint(jitter_key, (slots_total,), 0, 4096)
            ranking = (jitter_vals + (owners == forced).astype(jnp.int32) * 8192) * slots_total + slot_ids
            chosen = jnp.argsort(-ranking)[:endpoints]
            chosen_owner = (chosen // CAP).astype(jnp.int32)
            chosen_owner = chosen_owner[jax.random.permutation(order_key, endpoints)]
            offsets = jax.random.randint(offset_key, (endpoints,), 0, ROWS_DEV)
            row_ids = (chosen_owner * ROWS_DEV + offsets).reshape(P_DEV, 2)
            return jnp.stack([jnp.min(row_ids, axis=1), jnp.max(row_ids, axis=1)], axis=1)
        return jax.vmap(one_block)(block_keys).reshape(N_SEQ * P_DEV, 2)
    return jax.vmap(one_window)(window_keys).astype(jnp.int32)


def plant(values, stream_key, least, top_value):
    place = [jax.random.randint(jax.random.fold_in(stream_key, axis), (), 0, length) for axis, length in enumerate(values.shape)]
    widest = values.shape.index(max(values.shape))
    next_to = place[:widest] + [(place[widest] + 1) % values.shape[widest]] + place[widest + 1:]
    return values.at[tuple(place)].set(least).at[tuple(next_to)].set(top_value)


def block_scale(key, extent, pieces, smallest, largest):
    factor_of = 1.0
    for axis_at, shards_of in pieces:
        draws = jax.random.uniform(jax.random.fold_in(jax.random.fold_in(key, 6), axis_at), (shards_of,), jnp.float32, smallest / len(pieces), largest / len(pieces))
        factor_of = factor_of * jnp.repeat(jnp.exp(draws), extent[axis_at] // shards_of).reshape((-1,) + (1,) * (len(extent) - 1 - axis_at))
    return factor_of


def centred(rng, shape, deviation, most, cuts=(), kind=jnp.bfloat16):
    loudness = block_scale(rng, shape, cuts, -0.22, 0.18) if cuts else 1.0
    array = jax.random.normal(rng, shape, jnp.float32) * deviation * loudness
    return jnp.minimum(jnp.maximum(array, -most), most).astype(kind)


def setup_inputs(seed: int = 0) -> dict:
    streams_of = jax.random.split(jax.random.key(seed), 8)
    conv_input = centred(streams_of[0], (WINDOWS, LENGTH, D), 1.0, 6.0, ((0, 4), (1, 32)))
    pre_activation = centred(streams_of[1], (WINDOWS, LENGTH, D), 1.0, 6.0, ((0, 4), (1, 32), (2, 2)))
    track_gradient = centred(streams_of[2], (WINDOWS, LENGTH, D), 1.0, 6.0, ((0, 4), (1, 32), (2, 2)))
    kernel = centred(streams_of[3], (KW, D, D), (KW * D) ** -0.5, 0.09375, ((2, 2),))
    pair_rows = draw_pair_rows(jax.random.fold_in(streams_of[7], 71), 0)
    pair_count = plant(jax.random.randint(streams_of[5], (WINDOWS, N_SEQ), P_DEV // 2, P_DEV + 1), jax.random.fold_in(streams_of[5], 1), P_DEV // 2, P_DEV).astype(jnp.int32)
    pair_gradient = centred(streams_of[6], (WINDOWS, PAIRS, 2, D), 1.0, 6.0, ((0, 4), (1, 32), (3, 2)))
    return {"conv_input": conv_input, "pre_activation": pre_activation, "track_gradient": track_gradient, "kernel": kernel, "pair_rows": pair_rows, "pair_count": pair_count, "pair_gradient": pair_gradient}


root_half = 0.7071067811865476
inv_root_tau = 0.3989422804014327

def gelu_slope(values):
    normal_cdf = 0.5 * (1.0 + lax.erf(values * root_half))
    return normal_cdf + values * inv_root_tau * jnp.exp(-0.5 * values * values)

def reference(conv_input, pre_activation, track_gradient, kernel, pair_rows, pair_count, pair_gradient):
    tap_count = kernel.shape[0]
    reach_rows = tap_count // 2
    seq_length = track_gradient.shape[1]
    channels = track_gradient.shape[2]
    pair_total = pair_rows.shape[1]
    endpoints = 2 * pair_total
    kernel_sum = jnp.zeros((tap_count, channels, channels), jnp.float32)
    skip_list = []
    lower_list = []
    for window_id in range(WINDOWS):
        row_ids = pair_rows[window_id].reshape(endpoints).astype(jnp.int32)
        pair_index = jnp.arange(endpoints, dtype=jnp.int32) // 2
        limits = pair_count[window_id][pair_index // P_DEV]
        is_valid = pair_index % P_DEV < limits
        end_grads = pair_gradient[window_id].reshape(endpoints, channels).astype(jnp.float32)
        end_grads = jnp.where(is_valid[:, None], end_grads, jnp.zeros_like(end_grads))
        junction = jnp.zeros((seq_length, channels), jnp.float32).at[row_ids].add(end_grads)
        out_grad = track_gradient[window_id].astype(jnp.float32) + junction
        slope_grad = (out_grad * gelu_slope(pre_activation[window_id].astype(jnp.float32))).astype(jnp.bfloat16)
        padded = jnp.pad(slope_grad, ((reach_rows, reach_rows), (0, 0)))
        input_grad = jnp.zeros((seq_length, channels), jnp.float32)
        for position in range(tap_count):
            begin_row = 2 * reach_rows - position
            window_rows = padded[begin_row:begin_row + seq_length]
            input_grad = input_grad + jnp.dot(window_rows, kernel[position].T, preferred_element_type=jnp.float32)
            kernel_sum = kernel_sum.at[position].add(jnp.dot(conv_input[window_id].T, window_rows, preferred_element_type=jnp.float32))
        skip_list.append(input_grad.astype(jnp.bfloat16))
        lower_list.append(input_grad.reshape(seq_length // 2, 2, channels).sum(axis=1).astype(jnp.bfloat16))
    scale_factor = 1.0 / math.sqrt(WINDOWS * LENGTH)
    return (jnp.stack(skip_list), jnp.stack(lower_list), kernel_sum * scale_factor)
```

```python
import jax
import jax.numpy as jnp
from jax import lax
from jax.sharding import PartitionSpec as P

root_half = 0.7071067811865476
inv_root_tau = 0.3989422804014327


def extended(cells, sides, width):
    for axis, dim in sides:
        count = lax.axis_size(axis)
        ends = count - 1
        head = lax.slice_in_dim(cells, 0, width, axis=dim)
        tail = lax.slice_in_dim(cells, cells.shape[dim] - width, cells.shape[dim], axis=dim)
        cells = jnp.concatenate(
            [
                lax.ppermute(tail, axis, [(i, (i + 1) % count) for i in range(ends)]),
                cells,
                lax.ppermute(head, axis, [((i + 1) % count, i) for i in range(ends)]),
            ],
            axis=dim,
        )
    return cells


def gelu_slope(values):
    normal_cdf = 0.5 * (1.0 + lax.erf(values * root_half))
    return normal_cdf + values * inv_root_tau * jnp.exp(-0.5 * values * values)


def conv_rows(padded, kernel_part, begin_row, row_count, reach_rows):
    running = None
    for position in range(kernel_part.shape[0]):
        window_rows = lax.dynamic_slice_in_dim(
            padded, begin_row + 2 * reach_rows - position, row_count, 0
        )
        product = lax.dot_general(
            window_rows,
            kernel_part[position],
            (((1,), (1,)), ((), ())),
            preferred_element_type=jnp.float32,
        )
        running = product if running is None else running + product
    return running


def shards(
    conv_input, pre_activation, track_gradient, kernel, pair_rows, pair_count, pair_gradient
):
    local_rows = track_gradient.shape[1]
    width_local = track_gradient.shape[2]
    tap_count = kernel.shape[0]
    reach_rows = tap_count // 2
    seq_count = lax.axis_size("seq")
    pairs_local = pair_rows.shape[1]
    capacity = min(2 * pairs_local, 6 * pairs_local // seq_count)
    endpoints = 2 * pairs_local
    row_ids = pair_rows[0].reshape(endpoints)
    end_grads = pair_gradient[0].reshape(endpoints, width_local)
    is_valid = jnp.arange(endpoints, dtype=jnp.int32) // 2 < pair_count[0, 0]
    owners = row_ids // local_rows
    offsets = row_ids - owners * local_rows
    owner_hits = (owners[:, None] == jnp.arange(seq_count, dtype=jnp.int32)[None, :]).astype(
        jnp.int32
    )
    ranks = jnp.sum((jnp.cumsum(owner_hits, axis=0) - 1) * owner_hits, axis=1)
    slots = owners * capacity + ranks
    kept_grads = jnp.where(is_valid[:, None], end_grads, jnp.zeros_like(end_grads))
    send_grads = (
        jnp.zeros((seq_count * capacity, width_local), jnp.bfloat16).at[slots].set(kept_grads)
    )
    send_offsets = (
        jnp.full((seq_count * capacity,), local_rows, jnp.int32)
        .at[slots]
        .set(jnp.where(is_valid, offsets, local_rows))
    )
    got_grads, got_offsets = (
        lax.all_to_all(
            send_grads.reshape(seq_count, capacity, width_local),
            "seq",
            split_axis=0,
            concat_axis=0,
            tiled=True,
        ),
        lax.all_to_all(
            send_offsets.reshape(seq_count, capacity),
            "seq",
            split_axis=0,
            concat_axis=0,
            tiled=True,
        ),
    )
    out_grad = (
        track_gradient[0]
        .astype(jnp.float32)
        .at[got_offsets.reshape(seq_count * capacity)]
        .add(got_grads.reshape(seq_count * capacity, width_local).astype(jnp.float32), mode="drop")
    )
    slope_grad = (out_grad * gelu_slope(pre_activation[0].astype(jnp.float32))).astype(jnp.bfloat16)
    padded = extended(slope_grad, (("seq", 0),), 2)
    inputs_local = conv_input[0]
    kernel_pieces = []
    for position in range(tap_count):
        begin_row = 2 * reach_rows - position
        window_rows = padded[begin_row : begin_row + local_rows]
        kernel_pieces.append(
            lax.dot_general(
                inputs_local,
                window_rows,
                (((0,), (0,)), ((), ())),
                preferred_element_type=jnp.float32,
            )
        )
    kernel_local = jnp.stack(kernel_pieces)
    share_rows = local_rows // lax.axis_size("mp")
    input_grad = lax.psum_scatter(
        conv_rows(padded, kernel, jnp.int32(0), lax.axis_size("mp") * share_rows, reach_rows),
        "mp",
        scatter_dimension=0,
        tiled=True,
    )
    channels = input_grad.shape[1]
    grad_skip = input_grad.astype(jnp.bfloat16)[None]
    grad_lower = (
        input_grad.reshape(share_rows // 2, 2, channels).sum(axis=1).astype(jnp.bfloat16)[None]
    )
    total_rows = local_rows * seq_count * lax.axis_size("batch")
    scale_factor = total_rows ** (-0.5)
    channels_in = kernel_local.shape[1]
    piece_rows = channels_in // seq_count
    parts = kernel_local.astype(jnp.bfloat16).reshape(
        tap_count, seq_count, piece_rows, width_local
    )
    parts = lax.all_to_all(parts, "seq", split_axis=1, concat_axis=1, tiled=True)
    piece = jnp.sum(parts.astype(jnp.float32), axis=1)
    kernel_grad = lax.psum(piece, "batch")
    return (grad_skip, grad_lower, kernel_grad * scale_factor)


def solution(mesh):
    in_specs = (
        P("batch", "seq", None),
        P("batch", "seq", "mp"),
        P("batch", "seq", "mp"),
        P(None, None, "mp"),
        P("batch", "seq", None),
        P("batch", "seq"),
        P("batch", "seq", None, "mp"),
    )
    out_specs = (
        P("batch", ("seq", "mp"), None),
        P("batch", ("seq", "mp"), None),
        P(None, "seq", "mp"),
    )
    return jax.shard_map(shards, mesh=mesh, in_specs=in_specs, out_specs=out_specs, check_vma=False)
```

```python
import functools

import jax
import jax.numpy as jnp
from jax import lax
from jax.experimental import pallas as pl
from jax.experimental.pallas import tpu as pltpu
from jax.sharding import PartitionSpec as P

MESH = pl.DeviceIdType.MESH
F32 = jnp.float32
BF16 = jnp.bfloat16
root_half = 0.7071067811865476
inv_root_tau = 0.3989422804014327
TILE = 256
BORDER = 16
CHUNKS = 4
PACK = 4
SLOT_ROWS = 128


def gelu_slope(values):
    normal_cdf = 0.5 * (1.0 + lax.erf(values * root_half))
    return normal_cdf + values * inv_root_tau * jnp.exp(-0.5 * values * values)


def body(
    sizes,
    rows_ref, count_ref, pairs_ref, track_ref, pre_ref, conv_ref, kern_ref,
    skip_ref, lower_ref, weight_ref,
    pairs_v, slot_v, onehot_v, send_v, recv_v, soff_v, roff_v,
    track_v, pre_v, conv_v, convt_v, slope_f, grad_v, kfull_v,
    share_v, other_v, other_f, wins_v, acc_v,
    wb_v, wa_v, wsb_v, wrb_v, wown_v, wsc_v, wrc_v, wfin_v,
    skip_v, lower_v,
    load_sem, g_send, g_recv, o_send, o_recv, kx_send, kx_recv, kc_send, kc_recv,
    h_send, h_recv, m_send, m_recv, a_send, a_recv, b_send, b_recv,
    c_send, c_recv, d_send, d_recv, out_sem,
):
    n_seq, n_x, cap, rows_dev, width, depth, taps, scale = sizes
    n_chip = n_seq // 2
    n_z = n_chip // 2
    reach = taps // 2
    endpoints = pairs_ref.shape[0]
    share = rows_dev // 2
    tiles = rows_dev // TILE
    share_tiles = share // TILE
    chip_rows = depth // n_chip
    block = wb_v.shape[1]
    half = block // 2
    piece = half // n_x
    per_chunk = n_chip // CHUNKS
    chunk_rows = chip_rows * per_chunk
    quarter = depth // 4

    me = lax.axis_index("seq")
    mp = lax.axis_index("mp")
    xme = lax.axis_index("batch")
    core = lax.rem(me, 2)
    chip = me // 2
    yhi = chip // n_z
    zme = lax.rem(chip, n_z)
    twin = me + 1 - 2 * core

    def at_seq(target):
        return {"seq": target}

    up = {"seq": (lax.rem(yhi + mp, 2) * n_z + zme) * 2 + core, "mp": 1 - mp}
    down = {"seq": (lax.rem(yhi + 1 - mp, 2) * n_z + zme) * 2 + core, "mp": 1 - mp}

    loads = [
        pltpu.make_async_copy(pairs_ref, pairs_v, load_sem.at[0]),
        pltpu.make_async_copy(pre_ref, pre_v, load_sem.at[1]),
        pltpu.make_async_copy(track_ref, track_v, load_sem.at[2]),
        pltpu.make_async_copy(conv_ref, conv_v, load_sem.at[3]),
        pltpu.make_async_copy(kern_ref, kfull_v.at[:, :, pl.ds(0, width)], load_sem.at[4]),
    ]
    for load in loads:
        load.start()

    barrier = pltpu.get_barrier_semaphore()

    def greet(target):
        pl.semaphore_signal(barrier, inc=1, device_id=target, device_id_type=MESH)

    @pl.loop(1, n_seq)
    def _(step):
        greet(at_seq(lax.rem(me + step, n_seq)))

    @pl.loop(1, n_x)
    def _(step):
        peer = lax.rem(xme + step, n_x)
        greet({"batch": peer})
        greet({"seq": twin, "batch": peer})

    greet(up)
    greet(down)

    lane = lax.broadcasted_iota(jnp.int32, (1, endpoints), 1)
    rows = rows_ref[...]
    owner = rows // rows_dev
    offset = rows - owner * rows_dev
    owner = jnp.where(lane // 2 < count_ref[0, 0], owner, n_seq)
    hit = owner == lax.broadcasted_iota(jnp.int32, (n_seq, endpoints), 0)
    rank = hit.astype(jnp.int32)
    wide_lane = lax.broadcasted_iota(jnp.int32, (n_seq, endpoints), 1)
    shift = 1
    while shift < endpoints:
        rank = rank + jnp.where(wide_lane >= shift, pltpu.roll(rank, shift, 1), 0)
        shift *= 2
    slot_v[...] = jnp.where(hit, rank - 1, -1)
    kind = lax.broadcasted_iota(jnp.int32, (16, endpoints), 0)
    parts = jnp.where(kind == 0, offset // 64, jnp.where(kind == 1, lax.rem(offset, 64), 1))
    parts = parts.astype(F32).astype(BF16)

    loads[0].wait()
    pl.semaphore_wait(barrier, (n_seq - 1) + 2 * (n_x - 1) + 2)

    def grads_to(step):
        return pltpu.make_async_remote_copy(
            src_ref=send_v.at[step],
            dst_ref=recv_v.at[pl.ds(pl.multiple_of(step * cap, 16), cap)],
            send_sem=g_send.at[step],
            recv_sem=g_recv.at[step],
            device_id=at_seq(lax.rem(me + step, n_seq)),
            device_id_type=MESH,
        )

    def offsets_to(step):
        return pltpu.make_async_remote_copy(
            src_ref=soff_v.at[step],
            dst_ref=roff_v.at[step],
            send_sem=o_send.at[step],
            recv_sem=o_recv.at[step],
            device_id=at_seq(lax.rem(me + step, n_seq)),
            device_id_type=MESH,
        )

    def pack(first):
        for i in range(PACK):
            target = lax.rem(me + first + i, n_seq)
            slots = slot_v[pl.ds(target, 1), :]
            places = lax.broadcasted_iota(jnp.int32, (SLOT_ROWS, endpoints), 0)
            onehot_v[pl.ds(i * SLOT_ROWS, SLOT_ROWS), :] = jnp.where(
                slots == places, 1.0, 0.0
            ).astype(BF16)
        onehot = onehot_v[...]
        listed = jnp.dot(onehot, pairs_v[...], preferred_element_type=F32).astype(BF16)
        marks = lax.dot_general(
            parts, onehot, (((1,), (1,)), ((), ())), preferred_element_type=F32
        )
        where_to = jnp.where(marks[2:3] > 0.5, marks[0:1] * 64.0 + marks[1:2], -1.0)
        return listed, where_to

    def emit(first, begin):
        listed, where_to = pack(first)
        for i in range(PACK):
            some = listed[i * SLOT_ROWS : i * SLOT_ROWS + cap]
            place = jnp.broadcast_to(
                where_to[:, i * SLOT_ROWS : (i + 1) * SLOT_ROWS], (8, SLOT_ROWS)
            )
            if i < begin:
                recv_v[pl.ds(0, cap), :] = some
                roff_v[0] = place
            else:
                send_v[first + i] = some
                soff_v[first + i] = place
                offsets_to(first + i).start()
                grads_to(first + i).start()

    emit(0, 1)

    @pl.loop(1, n_seq // PACK)
    def _(turn):
        emit(turn * PACK, 0)

    def kernel_piece(index):
        return pl.ds(pl.multiple_of(index * quarter, 16), quarter)

    def kernel_across(way, target):
        return pltpu.make_async_remote_copy(
            src_ref=kern_ref.at[:, kernel_piece(2 * core + way), :],
            dst_ref=kfull_v.at[:, kernel_piece(2 * core + way), pl.ds(width, width)],
            send_sem=kx_send.at[way],
            recv_sem=kx_recv.at[way],
            device_id=target,
            device_id_type=MESH,
        )

    def kernel_twin(way, at_core):
        region = kfull_v.at[:, kernel_piece(2 * at_core + way), pl.ds(width, width)]
        return pltpu.make_async_remote_copy(
            src_ref=region,
            dst_ref=region,
            send_sem=kc_send.at[way],
            recv_sem=kc_recv.at[way],
            device_id=at_seq(twin),
            device_id_type=MESH,
        )

    kernel_across(0, up).start()
    kernel_across(1, down).start()

    loads[1].wait()
    loads[2].wait()

    @pl.loop(0, tiles)
    def _(tile):
        at = pl.ds(pl.multiple_of(tile * TILE, TILE), TILE)
        grad_v[at, :] = gelu_slope(pre_v[at, :].astype(F32))
        slope_f[pl.ds(pl.multiple_of(BORDER + tile * TILE, BORDER), TILE), :] = track_v[
            at, :
        ].astype(F32)

    loads[3].wait()

    @pl.loop(0, tiles)
    def _(tile):
        at = pl.ds(pl.multiple_of(tile * TILE, TILE), TILE)
        turned = conv_v[at, :].T
        for place in range(n_chip):
            source = place // per_chunk + CHUNKS * (place % per_chunk)
            convt_v[pl.ds(place * chip_rows, chip_rows), at] = turned[
                source * chip_rows : (source + 1) * chip_rows
            ]

    for way in range(2):
        kernel_across(way, up).wait_recv()
        kernel_twin(way, core).start()

    tile_lane = lax.broadcasted_iota(jnp.int32, (8, SLOT_ROWS), 1)

    def four_lists(first):
        p = [roff_v[first + i] for i in range(4)]
        one = pltpu.roll(p[1], 96, 1)
        two = pltpu.roll(p[2], 64, 1)
        three = pltpu.roll(p[3], 32, 1)
        return jnp.concatenate(
            [
                jnp.where(tile_lane < 96, p[0], one),
                jnp.where(tile_lane < 64, one, two),
                jnp.where(tile_lane < 32, two, three),
            ],
            axis=1,
        )[0:1]

    groups = [(first, 8) for first in range(0, n_seq - 8, 8)] + [(n_seq - 8, 4), (n_seq - 4, 4)]
    for first, many in groups:

        @pl.loop(max(first, 1), first + many)
        def _(step):
            offsets_to(step).wait_recv()
            grads_to(step).wait_recv()

        lists = jnp.concatenate([four_lists(first + i) for i in range(0, many, 4)], axis=1)

        @pl.loop(0, tiles)
        def _(tile, first=first, many=many, lists=lists):
            row = lax.broadcasted_iota(jnp.int32, (TILE, many * cap), 0) + tile * TILE
            onehot = jnp.where(row.astype(F32) == lists, 1.0, 0.0).astype(BF16)
            at = pl.ds(pl.multiple_of(BORDER + tile * TILE, BORDER), TILE)
            slope_f[at, :] += jnp.dot(
                onehot,
                recv_v[pl.ds(first * cap, many * cap), :],
                preferred_element_type=F32,
            )

    @pl.loop(0, tiles)
    def _(tile):
        at = pl.ds(pl.multiple_of(BORDER + tile * TILE, BORDER), TILE)
        from_at = pl.ds(pl.multiple_of(tile * TILE, TILE), TILE)
        slope_f[at, :] = (slope_f[at, :] * grad_v[from_at, :]).astype(BF16).astype(F32)

    low = pl.ds(BORDER - 8, 8)
    high = pl.ds(BORDER + rows_dev, 8)

    def halo(way, target):
        own = pl.ds(BORDER, 8) if way == 0 else pl.ds(BORDER + rows_dev - 8, 8)
        return pltpu.make_async_remote_copy(
            src_ref=slope_f.at[own],
            dst_ref=slope_f.at[high if way == 0 else low],
            send_sem=h_send.at[way],
            recv_sem=h_recv.at[way],
            device_id=at_seq(target),
            device_id_type=MESH,
        )

    before = lax.rem(me + n_seq - 1, n_seq)
    after = lax.rem(me + 1, n_seq)

    @pl.when(me > 0)
    def _():
        halo(0, before).start()

    @pl.when(me < n_seq - 1)
    def _():
        halo(1, after).start()

    theirs = (1 - mp) * share

    def share_to(index, begin, many):
        return pltpu.make_async_remote_copy(
            src_ref=share_v.at[pl.ds(begin, many)],
            dst_ref=other_v.at[pl.ds(begin, many)],
            send_sem=m_send.at[index],
            recv_sem=m_recv.at[index],
            device_id={"mp": 1 - mp},
            device_id_type=MESH,
        )

    shares = [(t, BORDER + t * TILE, TILE) for t in range(share_tiles)] + [
        (share_tiles, 0, BORDER),
        (share_tiles + 1, BORDER + share, BORDER),
    ]

    def cast_share(begin, many):
        share_v[pl.ds(begin, many), :] = slope_f[
            pl.ds(pl.multiple_of(theirs + begin, BORDER), many), :
        ].astype(BF16)

    for index, begin, many in shares[:share_tiles]:
        cast_share(begin, many)
        share_to(index, begin, many).start()

    def windows(tile):
        at = pl.ds(pl.multiple_of(tile * TILE, TILE), TILE)
        near = slope_f[pl.ds(pl.multiple_of(BORDER - 8 + tile * TILE, 8), TILE + 16), :]
        for tap in range(taps):
            begin = 8 + reach - tap
            wins_v[at, pl.ds(tap * width, width)] = near[begin : begin + TILE].astype(BF16)

    @pl.loop(1, tiles - 1)
    def _(tile):
        windows(tile)

    @pl.when(me < n_seq - 1)
    def _():
        halo(0, before).wait_recv()

    @pl.when(me == n_seq - 1)
    def _():
        slope_f[high, :] = jnp.zeros((8, width), F32)

    @pl.when(me > 0)
    def _():
        halo(1, after).wait_recv()

    @pl.when(me == 0)
    def _():
        slope_f[low, :] = jnp.zeros((8, width), F32)

    slope_f[pl.ds(0, 8), :] = jnp.zeros((8, width), F32)
    slope_f[pl.ds(BORDER + rows_dev + 8, 8), :] = jnp.zeros((8, width), F32)
    for index, begin, many in shares[share_tiles:]:
        cast_share(begin, many)
        share_to(index, begin, many).start()

    windows(0)
    windows(tiles - 1)

    def chunk_at(turn):
        return pl.ds(pl.multiple_of(turn * per_chunk, per_chunk), per_chunk)

    def to_twin(turn, at_core):
        region = (chunk_at(turn), pl.ds(pl.multiple_of((1 - at_core) * half, 16), half))
        return pltpu.make_async_remote_copy(
            src_ref=wb_v.at[region[0], region[1]],
            dst_ref=wa_v.at[region[0]],
            send_sem=a_send.at[turn],
            recv_sem=a_recv.at[turn],
            device_id=at_seq(twin),
            device_id_type=MESH,
        )

    def to_x(turn, step):
        peer = lax.rem(xme + step, n_x)
        return pltpu.make_async_remote_copy(
            src_ref=wsb_v.at[peer, chunk_at(turn)],
            dst_ref=wrb_v.at[step - 1, chunk_at(turn)],
            send_sem=b_send.at[step - 1, turn],
            recv_sem=b_recv.at[step - 1, turn],
            device_id={"batch": peer},
            device_id_type=MESH,
        )

    if block > taps * chip_rows:
        pad = block - taps * chip_rows
        wb_v[:, pl.ds(taps * chip_rows, pad), :] = jnp.zeros((n_chip, pad, width), BF16)

    @pl.loop(0, CHUNKS + 1)
    def _(turn):
        @pl.when(turn < CHUNKS)
        def _():
            lhs = convt_v[pl.ds(pl.multiple_of(turn * chunk_rows, 16), chunk_rows), :]
            product = jnp.dot(lhs, wins_v[...], preferred_element_type=F32)
            for place in range(per_chunk):
                for tap in range(taps):
                    wb_v[turn * per_chunk + place, pl.ds(tap * chip_rows, chip_rows), :] = product[
                        place * chip_rows : (place + 1) * chip_rows,
                        tap * width : (tap + 1) * width,
                    ].astype(BF16)
            to_twin(turn, core).start()

        @pl.when(turn > 0)
        def _():
            last = turn - 1
            to_twin(last, core).wait_recv()
            at = chunk_at(last)
            own_half = pl.multiple_of(core * half, 16)
            for q in range(n_x):
                total = wb_v[at, pl.ds(own_half + q * piece, piece), :].astype(F32) + wa_v[
                    at, pl.ds(q * piece, piece), :
                ].astype(F32)
                wsb_v[q, at] = total.astype(BF16)
            mine = pl.multiple_of(xme * piece, 16)
            wown_v[at] = wb_v[at, pl.ds(own_half + mine, piece), :].astype(F32) + wa_v[
                at, pl.ds(mine, piece), :
            ].astype(F32)
            for step in range(1, n_x):
                to_x(last, step).start()

    for way in range(2):
        kernel_twin(way, 1 - core).wait_recv()
    loads[4].wait()
    for index, begin, many in shares[share_tiles:]:
        share_to(index, begin, many).wait_recv()
        other_f[pl.ds(begin, many), :] = other_v[pl.ds(begin, many), :].astype(F32)
    for index, begin, many in shares[:share_tiles]:
        share_to(index, begin, many).wait_recv()
        other_f[pl.ds(begin, many), :] = other_v[pl.ds(begin, many), :].astype(F32)

    ours = mp * share
    pick = (
        lax.broadcasted_iota(jnp.int32, (TILE // 2, TILE), 1)
        == 2 * lax.broadcasted_iota(jnp.int32, (TILE // 2, TILE), 0)
    )
    pick = jnp.where(pick, 1.0, 0.0).astype(BF16)

    def outs(tile):
        at = pl.ds(pl.multiple_of(tile * TILE, TILE), TILE)
        low_at = pl.ds(pl.multiple_of(tile * (TILE // 2), TILE // 2), TILE // 2)
        return (
            pltpu.make_async_copy(skip_v.at[at], skip_ref.at[at], out_sem.at[tile]),
            pltpu.make_async_copy(
                lower_v.at[low_at], lower_ref.at[low_at], out_sem.at[share_tiles + tile]
            ),
        )

    def input_tile(tile):
        near = pl.multiple_of(BORDER - 8 + tile * TILE, 8)
        mine = slope_f[pl.ds(pl.multiple_of(ours + near, 8), TILE + 16), :]
        other = other_f[pl.ds(near, TILE + 16), :]
        for tap in range(taps):
            begin = 8 + reach - tap
            window = jnp.concatenate(
                [mine[begin : begin + TILE].astype(BF16), other[begin : begin + TILE].astype(BF16)],
                axis=1,
            )
            product = lax.dot_general(
                window, kfull_v[tap], (((1,), (1,)), ((), ())), preferred_element_type=F32
            )
            if tap == 0:
                acc_v[...] = product
            else:
                acc_v[...] += product
        total = acc_v[...]
        paired = (total + pltpu.roll(total, TILE - 1, 0)).astype(BF16)
        at = pl.ds(pl.multiple_of(tile * TILE, TILE), TILE)
        low_at = pl.ds(pl.multiple_of(tile * (TILE // 2), TILE // 2), TILE // 2)
        skip_v[at, :] = total.astype(BF16)
        lower_v[low_at, :] = jnp.dot(pick, paired, preferred_element_type=F32).astype(BF16)
        for copy in outs(tile):
            copy.start()

    def to_chip(target, slot):
        return pltpu.make_async_remote_copy(
            src_ref=wsc_v.at[target],
            dst_ref=wrc_v.at[slot],
            send_sem=c_send.at[slot],
            recv_sem=c_recv.at[slot],
            device_id=at_seq(2 * target + core),
            device_id_type=MESH,
        )

    def x_sum(turn):
        at = chunk_at(turn)
        for step in range(1, n_x):
            to_x(turn, step).wait_recv()
        total = wown_v[at]
        for step in range(1, n_x):
            total = total + wrb_v[step - 1, at].astype(F32)
        wown_v[at] = total
        for i in range(per_chunk):
            target = turn + CHUNKS * i
            wsc_v[target] = total[i].astype(BF16)

            @pl.when(target != chip)
            def _():
                to_chip(target, lax.rem(target - chip + n_chip, n_chip)).start()

    @pl.loop(0, CHUNKS)
    def _(turn):
        @pl.when(turn < share_tiles)
        def _():
            input_tile(turn)

        x_sum(turn)

    own_place = lax.rem(chip, CHUNKS) * per_chunk + chip // CHUNKS
    final = wown_v[own_place]
    for slot in range(1, n_chip):
        to_chip(chip, slot).wait_recv()
        final = final + wrc_v[slot].astype(F32)
    worker = core * n_x + xme
    wfin_v[worker] = final * scale

    def to_worker(index, target):
        return pltpu.make_async_remote_copy(
            src_ref=wfin_v.at[worker],
            dst_ref=wfin_v.at[worker],
            send_sem=d_send.at[index],
            recv_sem=d_recv.at[index],
            device_id=target,
            device_id_type=MESH,
        )

    def from_worker(index, who):
        return pltpu.make_async_remote_copy(
            src_ref=wfin_v.at[worker],
            dst_ref=wfin_v.at[who],
            send_sem=d_send.at[index],
            recv_sem=d_recv.at[index],
            device_id=at_seq(twin),
            device_id_type=MESH,
        )

    for step in range(n_x):
        peer = lax.rem(xme + step, n_x)
        to_worker(step, {"seq": twin, "batch": peer}).start()
        if step:
            to_worker(n_x + step, {"batch": peer}).start()
    for step in range(n_x):
        peer = lax.rem(xme + n_x - step, n_x)
        from_worker(step, (1 - core) * n_x + peer).wait_recv()
        if step:
            from_worker(n_x + step, core * n_x + peer).wait_recv()

    whole = wfin_v[...].reshape(block, width)
    upper = jnp.concatenate(
        [
            whole[tap * chip_rows : tap * chip_rows + chip_rows // 2][None]
            for tap in range(taps)
        ]
    )
    under = jnp.concatenate(
        [
            whole[tap * chip_rows + chip_rows // 2 : (tap + 1) * chip_rows][None]
            for tap in range(taps)
        ]
    )
    weight_ref[...] = jnp.where(core == 0, upper, under)

    for tile in range(share_tiles):
        for copy in outs(tile):
            copy.wait()

    @pl.loop(1, n_seq)
    def _(step):
        offsets_to(step).wait_send()
        grads_to(step).wait_send()

    for way in range(2):
        kernel_across(way, up).wait_send()
        kernel_twin(way, core).wait_send()

    @pl.when(me > 0)
    def _():
        halo(0, before).wait_send()

    @pl.when(me < n_seq - 1)
    def _():
        halo(1, after).wait_send()

    for index, begin, many in shares:
        share_to(index, begin, many).wait_send()
    for turn in range(CHUNKS):
        to_twin(turn, core).wait_send()
        for step in range(1, n_x):
            to_x(turn, step).wait_send()
    for slot in range(1, n_chip):
        to_chip(chip, slot).wait_send()
    for step in range(n_x):
        to_worker(step, at_seq(twin)).wait_send()
        if step:
            to_worker(n_x + step, at_seq(twin)).wait_send()


def shards(
    conv_input, pre_activation, track_gradient, kernel, pair_rows, pair_count, pair_gradient
):
    n_seq, n_x = lax.axis_size("seq"), lax.axis_size("batch")
    rows_dev, width = track_gradient.shape[1:]
    depth = conv_input.shape[2]
    taps = kernel.shape[0]
    pairs = pair_rows.shape[1]
    endpoints = 2 * pairs
    cap = min(endpoints, 6 * pairs // n_seq)
    n_chip = n_seq // 2
    share = rows_dev // 2
    share_tiles = share // TILE
    chip_rows = depth // n_chip
    unit = 32 * n_x
    block = -(-taps * chip_rows // unit) * unit
    half = block // 2
    piece = half // n_x
    scale = (rows_dev * n_seq * n_x) ** -0.5
    sizes = (n_seq, n_x, cap, rows_dev, width, depth, taps, scale)
    any_spec = pl.BlockSpec(memory_space=pl.ANY)
    vmem = pltpu.VMEM
    dma = pltpu.SemaphoreType.DMA
    skip, lower, weight = pl.pallas_call(
        functools.partial(body, sizes),
        out_shape=(
            jax.ShapeDtypeStruct((share, depth), BF16),
            jax.ShapeDtypeStruct((share // 2, depth), BF16),
            jax.ShapeDtypeStruct((taps, chip_rows // 2, width), F32),
        ),
        in_specs=[
            pl.BlockSpec(memory_space=pltpu.VMEM),
            pl.BlockSpec(memory_space=pltpu.SMEM),
        ]
        + [any_spec] * 5,
        out_specs=(any_spec, any_spec, pl.BlockSpec(memory_space=pltpu.VMEM)),
        scratch_shapes=[
            vmem((endpoints, width), BF16),
            vmem((n_seq, endpoints), jnp.int32),
            vmem((PACK * SLOT_ROWS, endpoints), BF16),
            vmem((n_seq, cap, width), BF16),
            vmem((n_seq * cap, width), BF16),
            vmem((n_seq, 8, SLOT_ROWS), F32),
            vmem((n_seq, 8, SLOT_ROWS), F32),
            vmem((rows_dev, width), BF16),
            vmem((rows_dev, width), BF16),
            vmem((rows_dev, depth), BF16),
            vmem((depth, rows_dev), BF16),
            vmem((rows_dev + 2 * BORDER, width), F32),
            vmem((rows_dev, width), F32),
            vmem((taps, depth, 2 * width), BF16),
            vmem((share + 2 * BORDER, width), BF16),
            vmem((share + 2 * BORDER, width), BF16),
            vmem((share + 2 * BORDER, width), F32),
            vmem((rows_dev, taps * width), BF16),
            vmem((TILE, depth), F32),
            vmem((n_chip, block, width), BF16),
            vmem((n_chip, half, width), BF16),
            vmem((n_x, n_chip, piece, width), BF16),
            vmem((n_x - 1, n_chip, piece, width), BF16),
            vmem((n_chip, piece, width), F32),
            vmem((n_chip, piece, width), BF16),
            vmem((n_chip, piece, width), BF16),
            vmem((2 * n_x, piece, width), F32),
            vmem((share, depth), BF16),
            vmem((share // 2, depth), BF16),
            dma((5,)),
            dma((n_seq,)),
            dma((n_seq,)),
            dma((n_seq,)),
            dma((n_seq,)),
            dma((2,)),
            dma((2,)),
            dma((2,)),
            dma((2,)),
            dma((2,)),
            dma((2,)),
            dma((share_tiles + 2,)),
            dma((share_tiles + 2,)),
            dma((CHUNKS,)),
            dma((CHUNKS,)),
            dma((n_x - 1, CHUNKS)),
            dma((n_x - 1, CHUNKS)),
            dma((n_chip,)),
            dma((n_chip,)),
            dma((2 * n_x,)),
            dma((2 * n_x,)),
            dma((2 * share_tiles,)),
        ],
        compiler_params=pltpu.CompilerParams(
            collective_id=0, has_side_effects=True, vmem_limit_bytes=63 * 1024 * 1024
        ),
    )(
        pair_rows[0].reshape(1, endpoints),
        pair_count,
        pair_gradient[0].reshape(endpoints, width),
        track_gradient[0],
        pre_activation[0],
        conv_input[0],
        kernel,
    )
    return skip[None], lower[None], weight


def solution(mesh):
    in_specs = (
        P("batch", "seq", None),
        P("batch", "seq", "mp"),
        P("batch", "seq", "mp"),
        P(None, None, "mp"),
        P("batch", "seq", None),
        P("batch", "seq"),
        P("batch", "seq", None, "mp"),
    )
    out_specs = (
        P("batch", ("seq", "mp"), None),
        P("batch", ("seq", "mp"), None),
        P(None, "seq", "mp"),
    )
    return jax.shard_map(shards, mesh=mesh, in_specs=in_specs, out_specs=out_specs, check_vma=False)
```

```python
import functools

import jax
import jax.numpy as jnp
from jax import lax
from jax.experimental import pallas as pl
from jax.experimental.pallas import tpu as pltpu
from jax.sharding import PartitionSpec as P

MESH = pl.DeviceIdType.MESH
F32 = jnp.float32
BF16 = jnp.bfloat16
root_half = 0.7071067811865476
inv_root_tau = 0.3989422804014327
TILE = 256
BORDER = 16
CHUNKS = 4
PACK = 4
SLOT_ROWS = 128
LANES = ((0, 256), (256, 128))


def gelu_slope(values):
    normal_cdf = 0.5 * (1.0 + lax.erf(values * root_half))
    return normal_cdf + values * inv_root_tau * jnp.exp(-0.5 * values * values)


def body(
    sizes,
    rows_ref, count_ref, pairs_ref, track_ref, pre_ref, conv_ref, kern_ref,
    skip_ref, lower_ref, weight_ref,
    raw_v, pairs_v, slot_v, onehot_v, send_v, recv_v, soff_v, roff_v,
    track_v, pre_v, conv_v, convt_v, slope_f, grad_v, kfull_v,
    share_v, other_v, other_f, wins_v, acc_v,
    wb_v, wa_v, wsb_v, wrb_v, wown_v, wsc_v, wrc_v, wfin_v,
    skip_v, lower_v,
    load_sem, g_send, g_recv, o_send, o_recv, kx_send, kx_recv, kc_send, kc_recv,
    h_send, h_recv, m_send, m_recv, a_send, a_recv, b_send, b_recv,
    c_send, c_recv, d_send, d_recv, out_sem,
):
    n_seq, n_x, cap, rows_dev, width, depth, taps, scale = sizes
    n_chip = n_seq // 2
    n_z = n_chip // 2
    reach = taps // 2
    endpoints = 2 * pairs_ref.shape[0]
    share = rows_dev // 2
    tiles = rows_dev // TILE
    share_tiles = share // TILE
    chip_rows = depth // n_chip
    block = wb_v.shape[1]
    half = block // 2
    piece = half // n_x
    per_chunk = n_chip // CHUNKS
    chunk_rows = chip_rows * per_chunk
    quarter = depth // 4

    me = lax.axis_index("seq")
    mp = lax.axis_index("mp")
    xme = lax.axis_index("batch")
    core = lax.rem(me, 2)
    chip = me // 2
    yhi = chip // n_z
    zme = lax.rem(chip, n_z)
    twin = me + 1 - 2 * core

    def at_seq(target):
        return {"seq": target}

    up = {"seq": (lax.rem(yhi + mp, 2) * n_z + zme) * 2 + core, "mp": 1 - mp}
    down = {"seq": (lax.rem(yhi + 1 - mp, 2) * n_z + zme) * 2 + core, "mp": 1 - mp}

    loads = [
        pltpu.make_async_copy(pairs_ref, raw_v, load_sem.at[0]),
        pltpu.make_async_copy(pre_ref, pre_v, load_sem.at[1]),
        pltpu.make_async_copy(track_ref, track_v, load_sem.at[2]),
        pltpu.make_async_copy(conv_ref, conv_v, load_sem.at[3]),
    ] + [
        pltpu.make_async_copy(
            kern_ref.at[:, :, pl.ds(lane, many)],
            kfull_v.at[:, :, pl.ds(2 * lane, many)],
            load_sem.at[4 + part],
        )
        for part, (lane, many) in enumerate(LANES)
    ]
    for load in loads:
        load.start()

    barrier = pltpu.get_barrier_semaphore()

    def greet(target):
        pl.semaphore_signal(barrier, inc=1, device_id=target, device_id_type=MESH)

    @pl.loop(1, n_seq)
    def _(step):
        greet(at_seq(lax.rem(me + step, n_seq)))

    @pl.loop(1, n_x)
    def _(step):
        peer = lax.rem(xme + step, n_x)
        greet({"batch": peer})
        greet({"seq": twin, "batch": peer})

    greet(up)
    greet(down)

    lane = lax.broadcasted_iota(jnp.int32, (1, endpoints), 1)
    rows = rows_ref[...]
    owner = rows // rows_dev
    offset = rows - owner * rows_dev
    owner = jnp.where(lane // 2 < count_ref[0, 0], owner, n_seq)
    hit = owner == lax.broadcasted_iota(jnp.int32, (n_seq, endpoints), 0)
    rank = hit.astype(jnp.int32)
    wide_lane = lax.broadcasted_iota(jnp.int32, (n_seq, endpoints), 1)
    shift = 1
    while shift < endpoints:
        rank = rank + jnp.where(wide_lane >= shift, pltpu.roll(rank, shift, 1), 0)
        shift *= 2
    slot_v[...] = jnp.where(hit, rank - 1, -1)
    kind = lax.broadcasted_iota(jnp.int32, (16, endpoints), 0)
    parts = jnp.where(kind == 0, offset // 64, jnp.where(kind == 1, lax.rem(offset, 64), 1))
    parts = parts.astype(F32).astype(BF16)

    loads[0].wait()
    pairs_v[...] = raw_v[...].reshape(endpoints, width)
    pl.semaphore_wait(barrier, (n_seq - 1) + 2 * (n_x - 1) + 2)

    def grads_to(part, step):
        lanes = pl.ds(*LANES[part])
        return pltpu.make_async_remote_copy(
            src_ref=send_v.at[step, :, lanes],
            dst_ref=recv_v.at[pl.ds(pl.multiple_of(step * cap, 16), cap), lanes],
            send_sem=g_send.at[part, step],
            recv_sem=g_recv.at[part, step],
            device_id=at_seq(lax.rem(me + step, n_seq)),
            device_id_type=MESH,
        )

    def offsets_to(step):
        return pltpu.make_async_remote_copy(
            src_ref=soff_v.at[step],
            dst_ref=roff_v.at[step],
            send_sem=o_send.at[step],
            recv_sem=o_recv.at[step],
            device_id=at_seq(lax.rem(me + step, n_seq)),
            device_id_type=MESH,
        )

    def pack(first):
        for i in range(PACK):
            target = lax.rem(me + first + i, n_seq)
            slots = slot_v[pl.ds(target, 1), :].astype(F32).astype(BF16)
            places = lax.broadcasted_iota(jnp.int32, (SLOT_ROWS, endpoints), 0)
            onehot_v[pl.ds(i * SLOT_ROWS, SLOT_ROWS), :] = jnp.where(
                slots == places.astype(F32).astype(BF16), jnp.ones((), BF16), jnp.zeros((), BF16)
            )
        onehot = onehot_v[...]
        listed = jnp.dot(onehot, pairs_v[...], preferred_element_type=F32).astype(BF16)
        marks = lax.dot_general(
            parts, onehot, (((1,), (1,)), ((), ())), preferred_element_type=F32
        )
        where_to = jnp.where(marks[2:3] > 0.5, marks[0:1] * 64.0 + marks[1:2], -1.0)
        return listed, where_to

    def emit(first, begin):
        listed, where_to = pack(first)
        for i in range(PACK):
            some = listed[i * SLOT_ROWS : i * SLOT_ROWS + cap]
            place = where_to[:, i * SLOT_ROWS : (i + 1) * SLOT_ROWS]
            if i < begin:
                recv_v[pl.ds(0, cap), :] = some
                roff_v[0] = place
            else:
                send_v[first + i] = some
                soff_v[first + i] = place
                offsets_to(first + i).start()
                grads_to(0, first + i).start()

    def kernel_piece(index):
        return pl.ds(pl.multiple_of(index * quarter, 16), quarter)

    def kernel_across(way, part, target):
        lane, many = LANES[part]
        rows_at = kernel_piece(2 * core + way)
        return pltpu.make_async_remote_copy(
            src_ref=kern_ref.at[:, rows_at, pl.ds(lane, many)],
            dst_ref=kfull_v.at[:, rows_at, pl.ds(2 * lane + many, many)],
            send_sem=kx_send.at[way, part],
            recv_sem=kx_recv.at[way, part],
            device_id=target,
            device_id_type=MESH,
        )

    def kernel_twin(way, part, at_core):
        lane, many = LANES[part]
        region = kfull_v.at[:, kernel_piece(2 * at_core + way), pl.ds(2 * lane + many, many)]
        return pltpu.make_async_remote_copy(
            src_ref=region,
            dst_ref=region,
            send_sem=kc_send.at[way, part],
            recv_sem=kc_recv.at[way, part],
            device_id=at_seq(twin),
            device_id_type=MESH,
        )

    halves = [(way, part) for part in range(len(LANES)) for way in range(2)]
    for way, part in halves:
        kernel_across(way, part, down if way else up).start()

    emit(0, 1)

    @pl.loop(1, n_seq // PACK)
    def _(turn):
        emit(turn * PACK, 0)

    for part in range(1, len(LANES)):

        @pl.loop(1, n_seq)
        def _(step):
            grads_to(part, step).start()

    loads[1].wait()
    loads[2].wait()

    @pl.loop(0, tiles)
    def _(tile):
        at = pl.ds(pl.multiple_of(tile * TILE, TILE), TILE)
        grad_v[at, :] = gelu_slope(pre_v[at, :].astype(F32))
        slope_f[pl.ds(pl.multiple_of(BORDER + tile * TILE, BORDER), TILE), :] = track_v[
            at, :
        ].astype(F32)

    loads[3].wait()

    @pl.loop(0, tiles)
    def _(tile):
        at = pl.ds(pl.multiple_of(tile * TILE, TILE), TILE)
        turned = conv_v[at, :].T
        for place in range(n_chip):
            source = place // per_chunk + CHUNKS * (place % per_chunk)
            convt_v[pl.ds(place * chip_rows, chip_rows), at] = turned[
                source * chip_rows : (source + 1) * chip_rows
            ]

    tile_lane = lax.broadcasted_iota(jnp.int32, (1, SLOT_ROWS), 1)

    def four_lists(first):
        p = [roff_v[first + i] for i in range(4)]
        one = pltpu.roll(p[1], 96, 1)
        two = pltpu.roll(p[2], 64, 1)
        three = pltpu.roll(p[3], 32, 1)
        return jnp.concatenate(
            [
                jnp.where(tile_lane < 96, p[0], one),
                jnp.where(tile_lane < 64, one, two),
                jnp.where(tile_lane < 32, two, three),
            ],
            axis=1,
        )

    groups = [(first, 8) for first in range(0, n_seq - 8, 8)] + [(n_seq - 8, 4), (n_seq - 4, 4)]
    before = lax.rem(me + n_seq - 1, n_seq)
    after = lax.rem(me + 1, n_seq)
    low = pl.ds(BORDER - 8, 8)
    high = pl.ds(BORDER + rows_dev, 8)
    theirs = (1 - mp) * share
    ours = mp * share
    last_part = len(LANES) - 1

    few_rows = lax.broadcasted_iota(jnp.int32, (16, 8 * cap), 0).astype(F32).astype(BF16)
    one, zero = jnp.ones((), BF16), jnp.zeros((), BF16)

    def junction(part, begin_group, end_group):
        lanes = pl.ds(*LANES[part])
        for first, many in groups[begin_group:end_group]:
            @pl.loop(max(first, 1), first + many)
            def _(step):
                if part == 0:
                    offsets_to(step).wait_recv()
                grads_to(part, step).wait_recv()

            lists = jnp.concatenate([four_lists(first + i) for i in range(0, many, 4)], axis=1)
            ends = first + many == n_seq

            @pl.loop(0, tiles)
            def _(tile, first=first, many=many, lists=lists, ends=ends):
                wanted = (lists - (tile * TILE).astype(F32)).astype(BF16)
                wanted = jnp.broadcast_to(wanted, (16, many * cap))
                onehot = jnp.concatenate(
                    [
                        jnp.where(wanted == few_rows[:, : many * cap] + 16.0 * i, one, zero)
                        for i in range(TILE // 16)
                    ]
                )
                at = pl.ds(pl.multiple_of(BORDER + tile * TILE, BORDER), TILE)
                total = slope_f[at, lanes] + jnp.dot(
                    onehot,
                    recv_v[pl.ds(first * cap, many * cap), lanes],
                    preferred_element_type=F32,
                )
                if ends:
                    slope = grad_v[pl.ds(pl.multiple_of(tile * TILE, TILE), TILE), lanes]
                    total = (total * slope).astype(BF16).astype(F32)
                slope_f[at, lanes] = total

    def halo(part, way, target):
        lanes = pl.ds(*LANES[part])
        own = pl.ds(BORDER, 8) if way == 0 else pl.ds(BORDER + rows_dev - 8, 8)
        return pltpu.make_async_remote_copy(
            src_ref=slope_f.at[own, lanes],
            dst_ref=slope_f.at[high if way == 0 else low, lanes],
            send_sem=h_send.at[part, way],
            recv_sem=h_recv.at[part, way],
            device_id=at_seq(target),
            device_id_type=MESH,
        )

    def share_to(part, index, begin, many):
        lanes = pl.ds(*LANES[part])
        return pltpu.make_async_remote_copy(
            src_ref=share_v.at[pl.ds(begin, many), lanes],
            dst_ref=other_v.at[pl.ds(begin, many), lanes],
            send_sem=m_send.at[part, index],
            recv_sem=m_recv.at[part, index],
            device_id={"mp": 1 - mp},
            device_id_type=MESH,
        )

    shares = [(t, BORDER + t * TILE, TILE) for t in range(share_tiles)] + [
        (share_tiles, 0, BORDER),
        (share_tiles + 1, BORDER + share, BORDER),
    ]

    def send_share(part, index, begin, many):
        lanes = pl.ds(*LANES[part])
        share_v[pl.ds(begin, many), lanes] = slope_f[
            pl.ds(pl.multiple_of(theirs + begin, BORDER), many), lanes
        ].astype(BF16)
        share_to(part, index, begin, many).start()

    def windows(part, tile):
        lane, many = LANES[part]
        at = pl.ds(pl.multiple_of(tile * TILE, TILE), TILE)
        near = slope_f[
            pl.ds(pl.multiple_of(BORDER - 8 + tile * TILE, 8), TILE + 16), pl.ds(lane, many)
        ]
        for tap in range(taps):
            begin = 8 + reach - tap
            wins_v[at, pl.ds(taps * lane + tap * many, many)] = near[
                begin : begin + TILE
            ].astype(BF16)

    def slopes_inner(part):
        @pl.when(me > 0)
        def _():
            halo(part, 0, before).start()

        @pl.when(me < n_seq - 1)
        def _():
            halo(part, 1, after).start()

        for index, begin, rows_many in shares[:share_tiles]:
            send_share(part, index, begin, rows_many)

        @pl.loop(1, tiles - 1)
        def _(tile):
            windows(part, tile)

    def slopes_outer(part):
        lanes = pl.ds(*LANES[part])
        many = LANES[part][1]

        @pl.when(me < n_seq - 1)
        def _():
            halo(part, 0, before).wait_recv()

        @pl.when(me == n_seq - 1)
        def _():
            slope_f[high, lanes] = jnp.zeros((8, many), F32)

        @pl.when(me > 0)
        def _():
            halo(part, 1, after).wait_recv()

        @pl.when(me == 0)
        def _():
            slope_f[low, lanes] = jnp.zeros((8, many), F32)

        for index, begin, rows_many in shares[share_tiles:]:
            send_share(part, index, begin, rows_many)
        windows(part, 0)
        windows(part, tiles - 1)

    def chunk_at(turn):
        return pl.ds(pl.multiple_of(turn * per_chunk, per_chunk), per_chunk)

    def to_twin(part, turn, at_core):
        lanes = pl.ds(*LANES[part])
        half_at = pl.ds(pl.multiple_of((1 - at_core) * half, 16), half)
        return pltpu.make_async_remote_copy(
            src_ref=wb_v.at[chunk_at(turn), half_at, lanes],
            dst_ref=wa_v.at[chunk_at(turn), :, lanes],
            send_sem=a_send.at[part, turn],
            recv_sem=a_recv.at[part, turn],
            device_id=at_seq(twin),
            device_id_type=MESH,
        )

    def to_x(part, turn, step):
        lanes = pl.ds(*LANES[part])
        peer = lax.rem(xme + step, n_x)
        return pltpu.make_async_remote_copy(
            src_ref=wsb_v.at[peer, chunk_at(turn), :, lanes],
            dst_ref=wrb_v.at[step - 1, chunk_at(turn), :, lanes],
            send_sem=b_send.at[part, step - 1, turn],
            recv_sem=b_recv.at[part, step - 1, turn],
            device_id={"batch": peer},
            device_id_type=MESH,
        )

    if block > taps * chip_rows:
        pad = block - taps * chip_rows
        wb_v[:, pl.ds(taps * chip_rows, pad), :] = jnp.zeros((n_chip, pad, width), BF16)

    def weights(part):
        lane, many = LANES[part]
        lanes = pl.ds(lane, many)

        @pl.loop(0, CHUNKS)
        def _(turn):
            lhs = convt_v[pl.ds(pl.multiple_of(turn * chunk_rows, 16), chunk_rows), :]
            product = jnp.dot(
                lhs,
                wins_v[:, pl.ds(taps * lane, taps * many)],
                preferred_element_type=F32,
            )
            for place in range(per_chunk):
                for tap in range(taps):
                    wb_v[turn * per_chunk + place, pl.ds(tap * chip_rows, chip_rows), lanes] = (
                        product[
                            place * chip_rows : (place + 1) * chip_rows,
                            tap * many : (tap + 1) * many,
                        ].astype(BF16)
                    )
            to_twin(part, turn, core).start()

    def twin_sum(part):
        lanes = pl.ds(*LANES[part])

        @pl.loop(0, CHUNKS)
        def _(turn):
            to_twin(part, turn, core).wait_recv()
            at = chunk_at(turn)
            own_half = pl.multiple_of(core * half, 16)
            for q in range(n_x):
                total = wb_v[at, pl.ds(own_half + q * piece, piece), lanes].astype(F32) + wa_v[
                    at, pl.ds(q * piece, piece), lanes
                ].astype(F32)
                wsb_v[q, at, :, lanes] = total.astype(BF16)
            for step in range(1, n_x):
                to_x(part, turn, step).start()
            mine = pl.multiple_of(xme * piece, 16)
            wown_v[at, :, lanes] = wb_v[at, pl.ds(own_half + mine, piece), lanes].astype(
                F32
            ) + wa_v[at, pl.ds(mine, piece), lanes].astype(F32)

    pick = (
        lax.broadcasted_iota(jnp.int32, (TILE // 2, TILE), 1)
        == 2 * lax.broadcasted_iota(jnp.int32, (TILE // 2, TILE), 0)
    )
    pick = jnp.where(pick, 1.0, 0.0).astype(BF16)

    def outs(tile):
        at = pl.ds(pl.multiple_of(tile * TILE, TILE), TILE)
        low_at = pl.ds(pl.multiple_of(tile * (TILE // 2), TILE // 2), TILE // 2)
        return (
            pltpu.make_async_copy(skip_v.at[at], skip_ref.at[at], out_sem.at[tile]),
            pltpu.make_async_copy(
                lower_v.at[low_at], lower_ref.at[low_at], out_sem.at[share_tiles + tile]
            ),
        )

    def take_shares(part):
        lanes = pl.ds(*LANES[part])
        for index, begin, many in shares:
            share_to(part, index, begin, many).wait_recv()
            other_f[pl.ds(begin, many), lanes] = other_v[pl.ds(begin, many), lanes].astype(F32)

    def input_tile(part, tile):
        lane, many = LANES[part]
        lanes = pl.ds(lane, many)
        near = pl.multiple_of(BORDER - 8 + tile * TILE, 8)
        at = pl.ds(pl.multiple_of(tile * TILE, TILE), TILE)
        mine = slope_f[pl.ds(pl.multiple_of(ours + near, 8), TILE + 16), lanes]
        other = other_f[pl.ds(near, TILE + 16), lanes]
        for tap in range(taps):
            begin = 8 + reach - tap
            window = jnp.concatenate(
                [mine[begin : begin + TILE].astype(BF16), other[begin : begin + TILE].astype(BF16)],
                axis=1,
            )
            product = lax.dot_general(
                window,
                kfull_v[tap, :, pl.ds(2 * lane, 2 * many)],
                (((1,), (1,)), ((), ())),
                preferred_element_type=F32,
            )
            if part == 0 and tap == 0:
                acc_v[at, :] = product
            else:
                acc_v[at, :] += product
        if part == last_part:
            total = acc_v[at, :]
            paired = (total + pltpu.roll(total, TILE - 1, 0)).astype(BF16)
            low_at = pl.ds(pl.multiple_of(tile * (TILE // 2), TILE // 2), TILE // 2)
            skip_v[at, :] = total.astype(BF16)
            lower_v[low_at, :] = jnp.dot(pick, paired, preferred_element_type=F32).astype(BF16)
            for copy in outs(tile):
                copy.start()

    def to_chip(part, target, slot):
        lanes = pl.ds(*LANES[part])
        return pltpu.make_async_remote_copy(
            src_ref=wsc_v.at[target, :, lanes],
            dst_ref=wrc_v.at[slot, :, lanes],
            send_sem=c_send.at[part, slot],
            recv_sem=c_recv.at[part, slot],
            device_id=at_seq(2 * target + core),
            device_id_type=MESH,
        )

    def x_sum(part, turn):
        lanes = pl.ds(*LANES[part])
        at = chunk_at(turn)
        for step in range(1, n_x):
            to_x(part, turn, step).wait_recv()
        total = wown_v[at, :, lanes]
        for step in range(1, n_x):
            total = total + wrb_v[step - 1, at, :, lanes].astype(F32)
        wown_v[at, :, lanes] = total
        for i in range(per_chunk):
            target = turn + CHUNKS * i
            wsc_v[target, :, lanes] = total[i].astype(BF16)

            @pl.when(target != chip)
            def _():
                to_chip(part, target, lax.rem(target - chip + n_chip, n_chip)).start()

    junction(0, 0, 5)
    slopes_inner(0)
    junction(1, 0, 1)
    slopes_outer(0)
    weights(0)
    for way, part in halves:
        kernel_across(way, part, up).wait_recv()
        kernel_twin(way, part, core).start()
    junction(1, 1, 2)
    twin_sum(0)
    junction(1, 2, 5)
    slopes_inner(1)

    @pl.loop(0, CHUNKS)
    def _(turn):
        x_sum(0, turn)

    slopes_outer(1)
    weights(1)
    twin_sum(1)
    for way, part in halves:
        kernel_twin(way, part, 1 - core).wait_recv()
    loads[4].wait()
    loads[5].wait()
    take_shares(0)

    @pl.loop(0, share_tiles)
    def _(tile):
        input_tile(0, tile)

    @pl.loop(0, CHUNKS)
    def _(turn):
        x_sum(1, turn)

    take_shares(1)

    @pl.loop(0, share_tiles)
    def _(tile):
        input_tile(1, tile)

    own_place = lax.rem(chip, CHUNKS) * per_chunk + chip // CHUNKS
    final = wown_v[own_place]
    for slot in range(1, n_chip):
        for part in range(len(LANES)):
            to_chip(part, chip, slot).wait_recv()
        final = final + wrc_v[slot].astype(F32)
    worker = core * n_x + xme
    wfin_v[worker] = final * scale

    def to_worker(index, target):
        return pltpu.make_async_remote_copy(
            src_ref=wfin_v.at[worker],
            dst_ref=wfin_v.at[worker],
            send_sem=d_send.at[index],
            recv_sem=d_recv.at[index],
            device_id=target,
            device_id_type=MESH,
        )

    def from_worker(index, who):
        return pltpu.make_async_remote_copy(
            src_ref=wfin_v.at[worker],
            dst_ref=wfin_v.at[who],
            send_sem=d_send.at[index],
            recv_sem=d_recv.at[index],
            device_id=at_seq(twin),
            device_id_type=MESH,
        )

    for step in range(n_x):
        peer = lax.rem(xme + step, n_x)
        to_worker(step, {"seq": twin, "batch": peer}).start()
        if step:
            to_worker(n_x + step, {"batch": peer}).start()
    for step in range(n_x):
        peer = lax.rem(xme + n_x - step, n_x)
        from_worker(step, (1 - core) * n_x + peer).wait_recv()
        if step:
            from_worker(n_x + step, core * n_x + peer).wait_recv()

    whole = wfin_v[...].reshape(block, width)
    upper = jnp.concatenate(
        [
            whole[tap * chip_rows : tap * chip_rows + chip_rows // 2][None]
            for tap in range(taps)
        ]
    )
    under = jnp.concatenate(
        [
            whole[tap * chip_rows + chip_rows // 2 : (tap + 1) * chip_rows][None]
            for tap in range(taps)
        ]
    )
    weight_ref[...] = jnp.where(core == 0, upper, under)

    for tile in range(share_tiles):
        for copy in outs(tile):
            copy.wait()

    @pl.loop(1, n_seq)
    def _(step):
        offsets_to(step).wait_send()
        for part in range(len(LANES)):
            grads_to(part, step).wait_send()

    for way, part in halves:
        kernel_across(way, part, up).wait_send()
        kernel_twin(way, part, core).wait_send()
    for part in range(len(LANES)):

        @pl.when(me > 0)
        def _():
            halo(part, 0, before).wait_send()

        @pl.when(me < n_seq - 1)
        def _():
            halo(part, 1, after).wait_send()

        for index, begin, many in shares:
            share_to(part, index, begin, many).wait_send()
        for turn in range(CHUNKS):
            to_twin(part, turn, core).wait_send()
            for step in range(1, n_x):
                to_x(part, turn, step).wait_send()
        for slot in range(1, n_chip):
            to_chip(part, chip, slot).wait_send()
    for step in range(n_x):
        to_worker(step, at_seq(twin)).wait_send()
        if step:
            to_worker(n_x + step, at_seq(twin)).wait_send()


def hand_over(skip_ref, lower_ref, weight_ref, skip_out, lower_out, weight_out):
    skip_out[...] = skip_ref[...]
    lower_out[...] = lower_ref[...]
    weight_out[...] = weight_ref[...]


def shards(
    conv_input, pre_activation, track_gradient, kernel, pair_rows, pair_count, pair_gradient
):
    n_seq, n_x = lax.axis_size("seq"), lax.axis_size("batch")
    rows_dev, width = track_gradient.shape[1:]
    depth = conv_input.shape[2]
    taps = kernel.shape[0]
    pairs = pair_rows.shape[1]
    endpoints = 2 * pairs
    cap = min(endpoints, 6 * pairs // n_seq)
    n_chip = n_seq // 2
    share = rows_dev // 2
    share_tiles = share // TILE
    chip_rows = depth // n_chip
    unit = 32 * n_x
    block = -(-taps * chip_rows // unit) * unit
    half = block // 2
    piece = half // n_x
    scale = (rows_dev * n_seq * n_x) ** -0.5
    sizes = (n_seq, n_x, cap, rows_dev, width, depth, taps, scale)
    any_spec = pl.BlockSpec(memory_space=pl.ANY)
    vmem = pltpu.VMEM
    dma = pltpu.SemaphoreType.DMA
    skip, lower, weight = pl.pallas_call(
        functools.partial(body, sizes),
        out_shape=(
            jax.ShapeDtypeStruct((share, depth), BF16),
            jax.ShapeDtypeStruct((share // 2, depth), BF16),
            jax.ShapeDtypeStruct((taps, chip_rows // 2, width), F32),
        ),
        in_specs=[
            pl.BlockSpec(memory_space=pltpu.VMEM),
            pl.BlockSpec(memory_space=pltpu.SMEM),
        ]
        + [any_spec] * 5,
        out_specs=(any_spec, any_spec, pl.BlockSpec(memory_space=pltpu.VMEM)),
        scratch_shapes=[
            vmem((pairs, 2, width), BF16),
            vmem((endpoints, width), BF16),
            vmem((n_seq, endpoints), jnp.int32),
            vmem((PACK * SLOT_ROWS, endpoints), BF16),
            vmem((n_seq, cap, width), BF16),
            vmem((n_seq * cap, width), BF16),
            vmem((n_seq, 1, SLOT_ROWS), F32),
            vmem((n_seq, 1, SLOT_ROWS), F32),
            vmem((rows_dev, width), BF16),
            vmem((rows_dev, width), BF16),
            vmem((rows_dev, depth), BF16),
            vmem((depth, rows_dev), BF16),
            vmem((rows_dev + 2 * BORDER, width), F32),
            vmem((rows_dev, width), F32),
            vmem((taps, depth, 2 * width), BF16),
            vmem((share + 2 * BORDER, width), BF16),
            vmem((share + 2 * BORDER, width), BF16),
            vmem((share + 2 * BORDER, width), F32),
            vmem((rows_dev, taps * width), BF16),
            vmem((share, depth), F32),
            vmem((n_chip, block, width), BF16),
            vmem((n_chip, half, width), BF16),
            vmem((n_x, n_chip, piece, width), BF16),
            vmem((n_x - 1, n_chip, piece, width), BF16),
            vmem((n_chip, piece, width), F32),
            vmem((n_chip, piece, width), BF16),
            vmem((n_chip, piece, width), BF16),
            vmem((2 * n_x, piece, width), F32),
            vmem((share, depth), BF16),
            vmem((share // 2, depth), BF16),
            dma((6,)),
            dma((2, n_seq)),
            dma((2, n_seq)),
            dma((n_seq,)),
            dma((n_seq,)),
            dma((2, 2)),
            dma((2, 2)),
            dma((2, 2)),
            dma((2, 2)),
            dma((2, 2)),
            dma((2, 2)),
            dma((2, share_tiles + 2)),
            dma((2, share_tiles + 2)),
            dma((2, CHUNKS)),
            dma((2, CHUNKS)),
            dma((2, n_x - 1, CHUNKS)),
            dma((2, n_x - 1, CHUNKS)),
            dma((2, n_chip)),
            dma((2, n_chip)),
            dma((2 * n_x,)),
            dma((2 * n_x,)),
            dma((2 * share_tiles,)),
        ],
        compiler_params=pltpu.CompilerParams(
            collective_id=0, has_side_effects=True, vmem_limit_bytes=63 * 1024 * 1024
        ),
    )(
        pair_rows[0].reshape(1, endpoints),
        pair_count,
        pair_gradient[0],
        track_gradient[0],
        pre_activation[0],
        conv_input[0],
        kernel,
    )
    steps = 4
    specs = (
        pl.BlockSpec((share // steps, depth), lambda i: (i, 0)),
        pl.BlockSpec((share // 2 // steps, depth), lambda i: (i, 0)),
        pl.BlockSpec((taps, chip_rows // 2, width), lambda i: (0, 0, 0)),
    )
    skip, lower, weight = pl.pallas_call(
        hand_over,
        grid=(steps,),
        out_shape=tuple(jax.ShapeDtypeStruct(a.shape, a.dtype) for a in (skip, lower, weight)),
        in_specs=specs,
        out_specs=specs,
    )(skip, lower, weight)
    return skip[None], lower[None], weight


def solution(mesh):
    in_specs = (
        P("batch", "seq", None),
        P("batch", "seq", "mp"),
        P("batch", "seq", "mp"),
        P(None, None, "mp"),
        P("batch", "seq", None),
        P("batch", "seq"),
        P("batch", "seq", None, "mp"),
    )
    out_specs = (
        P("batch", ("seq", "mp"), None),
        P("batch", ("seq", "mp"), None),
        P(None, "seq", "mp"),
    )
    return jax.shard_map(shards, mesh=mesh, in_specs=in_specs, out_specs=out_specs, check_vma=False)
```

```python
import functools

import jax
import jax.numpy as jnp
from jax import lax
from jax.experimental import pallas as pl
from jax.experimental.pallas import tpu as pltpu
from jax.sharding import PartitionSpec as P

MESH = pl.DeviceIdType.MESH
F32 = jnp.float32
BF16 = jnp.bfloat16
root_half = 0.7071067811865476
inv_root_tau = 0.3989422804014327
TILE = 256
BORDER = 16
CHUNKS = 4
PACK = 4
SLOT_ROWS = 128
LANES = ((0, 256), (256, 128))


def gelu_slope(values):
    normal_cdf = 0.5 * (1.0 + lax.erf(values * root_half))
    return normal_cdf + values * inv_root_tau * jnp.exp(-0.5 * values * values)


def body(
    sizes,
    rows_ref, count_ref, pairs_ref, track_ref, pre_ref, conv_ref, kern_ref,
    skip_ref, lower_ref, weight_ref,
    raw_v, pairs_v, slot_v, onehot_v, send_v, recv_v, soff_v, roff_v,
    track_v, pre_v, conv_v, convt_v, slope_f, grad_v, kfull_v,
    share_v, other_v, other_f, wins_v, acc_v,
    wb_v, wa_v, wsb_v, wrb_v, wown_v, wsc_v, wrc_v, wfin_v,
    skip_v, lower_v,
    load_sem, g_send, g_recv, o_send, o_recv, kx_send, kx_recv, kc_send, kc_recv,
    h_send, h_recv, m_send, m_recv, a_send, a_recv, b_send, b_recv,
    c_send, c_recv, d_send, d_recv, out_sem,
):
    n_seq, n_x, cap, rows_dev, width, depth, taps, scale = sizes
    n_chip = n_seq // 2
    n_z = n_chip // 2
    reach = taps // 2
    endpoints = 2 * pairs_ref.shape[0]
    share = rows_dev // 2
    tiles = rows_dev // TILE
    share_tiles = share // TILE
    chip_rows = depth // n_chip
    block = wb_v.shape[1]
    half = block // 2
    piece = half // n_x
    per_chunk = n_chip // CHUNKS
    chunk_rows = chip_rows * per_chunk
    quarter = depth // 4

    me = lax.axis_index("seq")
    mp = lax.axis_index("mp")
    xme = lax.axis_index("batch")
    core = lax.rem(me, 2)
    chip = me // 2
    yhi = chip // n_z
    zme = lax.rem(chip, n_z)
    twin = me + 1 - 2 * core

    def at_seq(target):
        return {"seq": target}

    up = {"seq": (lax.rem(yhi + mp, 2) * n_z + zme) * 2 + core, "mp": 1 - mp}
    down = {"seq": (lax.rem(yhi + 1 - mp, 2) * n_z + zme) * 2 + core, "mp": 1 - mp}

    loads = [
        pltpu.make_async_copy(pairs_ref, raw_v, load_sem.at[0]),
        pltpu.make_async_copy(pre_ref, pre_v, load_sem.at[1]),
        pltpu.make_async_copy(track_ref, track_v, load_sem.at[2]),
        pltpu.make_async_copy(conv_ref, conv_v, load_sem.at[3]),
    ] + [
        pltpu.make_async_copy(
            kern_ref.at[:, :, pl.ds(lane, many)],
            kfull_v.at[:, :, pl.ds(2 * lane, many)],
            load_sem.at[4 + part],
        )
        for part, (lane, many) in enumerate(LANES)
    ]
    for load in loads:
        load.start()

    barrier = pltpu.get_barrier_semaphore()

    def greet(target):
        pl.semaphore_signal(barrier, inc=1, device_id=target, device_id_type=MESH)

    @pl.loop(1, n_seq)
    def _(step):
        greet(at_seq(lax.rem(me + step, n_seq)))

    @pl.loop(1, n_x)
    def _(step):
        peer = lax.rem(xme + step, n_x)
        greet({"batch": peer})
        greet({"seq": twin, "batch": peer})

    greet(up)
    greet(down)

    lane = lax.broadcasted_iota(jnp.int32, (1, endpoints), 1)
    rows = rows_ref[...]
    owner = rows // rows_dev
    offset = rows - owner * rows_dev
    owner = jnp.where(lane // 2 < count_ref[0, 0], owner, n_seq)
    hit = owner == lax.broadcasted_iota(jnp.int32, (n_seq, endpoints), 0)
    rank = hit.astype(jnp.int32)
    wide_lane = lax.broadcasted_iota(jnp.int32, (n_seq, endpoints), 1)
    shift = 1
    while shift < endpoints:
        rank = rank + jnp.where(wide_lane >= shift, pltpu.roll(rank, shift, 1), 0)
        shift *= 2
    slot_v[...] = jnp.where(hit, rank - 1, -1)
    kind = lax.broadcasted_iota(jnp.int32, (16, endpoints), 0)
    parts = jnp.where(kind == 0, offset // 64, jnp.where(kind == 1, lax.rem(offset, 64), 1))
    parts = parts.astype(F32).astype(BF16)

    loads[0].wait()
    pairs_v[...] = raw_v[...].reshape(endpoints, width)
    pl.semaphore_wait(barrier, (n_seq - 1) + 2 * (n_x - 1) + 2)

    def grads_to(part, step):
        lanes = pl.ds(*LANES[part])
        return pltpu.make_async_remote_copy(
            src_ref=send_v.at[step, :, lanes],
            dst_ref=recv_v.at[pl.ds(pl.multiple_of(step * cap, 16), cap), lanes],
            send_sem=g_send.at[part, step],
            recv_sem=g_recv.at[part, step],
            device_id=at_seq(lax.rem(me + step, n_seq)),
            device_id_type=MESH,
        )

    def offsets_to(step):
        return pltpu.make_async_remote_copy(
            src_ref=soff_v.at[step],
            dst_ref=roff_v.at[step],
            send_sem=o_send.at[step],
            recv_sem=o_recv.at[step],
            device_id=at_seq(lax.rem(me + step, n_seq)),
            device_id_type=MESH,
        )

    def pack(first):
        for i in range(PACK):
            target = lax.rem(me + first + i, n_seq)
            slots = slot_v[pl.ds(target, 1), :].astype(F32).astype(BF16)
            places = lax.broadcasted_iota(jnp.int32, (SLOT_ROWS, endpoints), 0)
            onehot_v[pl.ds(i * SLOT_ROWS, SLOT_ROWS), :] = jnp.where(
                slots == places.astype(F32).astype(BF16), jnp.ones((), BF16), jnp.zeros((), BF16)
            )
        onehot = onehot_v[...]
        listed = jnp.dot(onehot, pairs_v[...], preferred_element_type=F32).astype(BF16)
        marks = lax.dot_general(
            parts, onehot, (((1,), (1,)), ((), ())), preferred_element_type=F32
        )
        where_to = jnp.where(marks[2:3] > 0.5, marks[0:1] * 64.0 + marks[1:2], -1.0)
        return listed, where_to

    def emit(first, begin):
        listed, where_to = pack(first)
        for i in range(PACK):
            some = listed[i * SLOT_ROWS : i * SLOT_ROWS + cap]
            place = where_to[:, i * SLOT_ROWS : (i + 1) * SLOT_ROWS]
            if i < begin:
                recv_v[pl.ds(0, cap), :] = some
                roff_v[0] = place
            else:
                send_v[first + i] = some
                soff_v[first + i] = place
                offsets_to(first + i).start()
                grads_to(0, first + i).start()

    def kernel_piece(index):
        return pl.ds(pl.multiple_of(index * quarter, 16), quarter)

    def kernel_across(way, part, target):
        lane, many = LANES[part]
        rows_at = kernel_piece(2 * core + way)
        return pltpu.make_async_remote_copy(
            src_ref=kern_ref.at[:, rows_at, pl.ds(lane, many)],
            dst_ref=kfull_v.at[:, rows_at, pl.ds(2 * lane + many, many)],
            send_sem=kx_send.at[way, part],
            recv_sem=kx_recv.at[way, part],
            device_id=target,
            device_id_type=MESH,
        )

    def kernel_twin(way, part, at_core):
        lane, many = LANES[part]
        region = kfull_v.at[:, kernel_piece(2 * at_core + way), pl.ds(2 * lane + many, many)]
        return pltpu.make_async_remote_copy(
            src_ref=region,
            dst_ref=region,
            send_sem=kc_send.at[way, part],
            recv_sem=kc_recv.at[way, part],
            device_id=at_seq(twin),
            device_id_type=MESH,
        )

    halves = [(way, part) for part in range(len(LANES)) for way in range(2)]
    for way, part in halves:
        kernel_across(way, part, down if way else up).start()

    emit(0, 1)

    @pl.loop(1, n_seq // PACK)
    def _(turn):
        emit(turn * PACK, 0)

    for part in range(1, len(LANES)):

        @pl.loop(1, n_seq)
        def _(step):
            grads_to(part, step).start()

    loads[1].wait()
    loads[2].wait()

    @pl.loop(0, tiles)
    def _(tile):
        at = pl.ds(pl.multiple_of(tile * TILE, TILE), TILE)
        grad_v[at, :] = gelu_slope(pre_v[at, :].astype(F32))
        slope_f[pl.ds(pl.multiple_of(BORDER + tile * TILE, BORDER), TILE), :] = track_v[
            at, :
        ].astype(F32)

    loads[3].wait()

    @pl.loop(0, tiles)
    def _(tile):
        at = pl.ds(pl.multiple_of(tile * TILE, TILE), TILE)
        turned = conv_v[at, :].T
        for place in range(n_chip):
            source = place // per_chunk + CHUNKS * (place % per_chunk)
            convt_v[pl.ds(place * chip_rows, chip_rows), at] = turned[
                source * chip_rows : (source + 1) * chip_rows
            ]

    tile_lane = lax.broadcasted_iota(jnp.int32, (1, SLOT_ROWS), 1)

    def four_lists(first):
        p = [roff_v[first + i] for i in range(4)]
        one = pltpu.roll(p[1], 96, 1)
        two = pltpu.roll(p[2], 64, 1)
        three = pltpu.roll(p[3], 32, 1)
        return jnp.concatenate(
            [
                jnp.where(tile_lane < 96, p[0], one),
                jnp.where(tile_lane < 64, one, two),
                jnp.where(tile_lane < 32, two, three),
            ],
            axis=1,
        )

    groups = [(first, 8) for first in range(0, n_seq - 8, 8)] + [(n_seq - 8, 4), (n_seq - 4, 4)]
    before = lax.rem(me + n_seq - 1, n_seq)
    after = lax.rem(me + 1, n_seq)
    low = pl.ds(BORDER - 8, 8)
    high = pl.ds(BORDER + rows_dev, 8)
    theirs = (1 - mp) * share
    ours = mp * share
    last_part = len(LANES) - 1

    few_rows = lax.broadcasted_iota(jnp.int32, (16, 8 * cap), 0).astype(F32).astype(BF16)
    one, zero = jnp.ones((), BF16), jnp.zeros((), BF16)

    def junction(part, begin_group, end_group):
        lanes = pl.ds(*LANES[part])
        for first, many in groups[begin_group:end_group]:
            @pl.loop(max(first, 1), first + many)
            def _(step):
                if part == 0:
                    offsets_to(step).wait_recv()
                grads_to(part, step).wait_recv()

            lists = jnp.concatenate([four_lists(first + i) for i in range(0, many, 4)], axis=1)
            ends = first + many == n_seq

            @pl.loop(0, tiles, unroll=4)
            def _(tile, first=first, many=many, lists=lists, ends=ends):
                wanted = (lists - (tile * TILE).astype(F32)).astype(BF16)
                wanted = jnp.broadcast_to(wanted, (16, many * cap))
                onehot = jnp.concatenate(
                    [
                        jnp.where(wanted == few_rows[:, : many * cap] + 16.0 * i, one, zero)
                        for i in range(TILE // 16)
                    ]
                )
                at = pl.ds(pl.multiple_of(BORDER + tile * TILE, BORDER), TILE)
                total = slope_f[at, lanes] + jnp.dot(
                    onehot,
                    recv_v[pl.ds(first * cap, many * cap), lanes],
                    preferred_element_type=F32,
                )
                if ends:
                    slope = grad_v[pl.ds(pl.multiple_of(tile * TILE, TILE), TILE), lanes]
                    total = (total * slope).astype(BF16).astype(F32)
                slope_f[at, lanes] = total

    def halo(part, way, target):
        lanes = pl.ds(*LANES[part])
        own = pl.ds(BORDER, 8) if way == 0 else pl.ds(BORDER + rows_dev - 8, 8)
        return pltpu.make_async_remote_copy(
            src_ref=slope_f.at[own, lanes],
            dst_ref=slope_f.at[high if way == 0 else low, lanes],
            send_sem=h_send.at[part, way],
            recv_sem=h_recv.at[part, way],
            device_id=at_seq(target),
            device_id_type=MESH,
        )

    def share_to(part, index, begin, many):
        lanes = pl.ds(*LANES[part])
        return pltpu.make_async_remote_copy(
            src_ref=share_v.at[pl.ds(begin, many), lanes],
            dst_ref=other_v.at[pl.ds(begin, many), lanes],
            send_sem=m_send.at[part, index],
            recv_sem=m_recv.at[part, index],
            device_id={"mp": 1 - mp},
            device_id_type=MESH,
        )

    shares = [(t, BORDER + t * TILE, TILE) for t in range(share_tiles)] + [
        (share_tiles, 0, BORDER),
        (share_tiles + 1, BORDER + share, BORDER),
    ]

    def send_share(part, index, begin, many):
        lanes = pl.ds(*LANES[part])
        share_v[pl.ds(begin, many), lanes] = slope_f[
            pl.ds(pl.multiple_of(theirs + begin, BORDER), many), lanes
        ].astype(BF16)
        share_to(part, index, begin, many).start()

    def windows(part, tile):
        lane, many = LANES[part]
        at = pl.ds(pl.multiple_of(tile * TILE, TILE), TILE)
        near = slope_f[
            pl.ds(pl.multiple_of(BORDER - 8 + tile * TILE, 8), TILE + 16), pl.ds(lane, many)
        ]
        for tap in range(taps):
            begin = 8 + reach - tap
            wins_v[at, pl.ds(taps * lane + tap * many, many)] = near[
                begin : begin + TILE
            ].astype(BF16)

    def slopes_inner(part):
        @pl.when(me > 0)
        def _():
            halo(part, 0, before).start()

        @pl.when(me < n_seq - 1)
        def _():
            halo(part, 1, after).start()

        for index, begin, rows_many in shares[:share_tiles]:
            send_share(part, index, begin, rows_many)

        @pl.loop(1, tiles - 1)
        def _(tile):
            windows(part, tile)

    def slopes_outer(part):
        lanes = pl.ds(*LANES[part])
        many = LANES[part][1]

        @pl.when(me < n_seq - 1)
        def _():
            halo(part, 0, before).wait_recv()

        @pl.when(me == n_seq - 1)
        def _():
            slope_f[high, lanes] = jnp.zeros((8, many), F32)

        @pl.when(me > 0)
        def _():
            halo(part, 1, after).wait_recv()

        @pl.when(me == 0)
        def _():
            slope_f[low, lanes] = jnp.zeros((8, many), F32)

        for index, begin, rows_many in shares[share_tiles:]:
            send_share(part, index, begin, rows_many)
        windows(part, 0)
        windows(part, tiles - 1)

    def chunk_at(turn):
        return pl.ds(pl.multiple_of(turn * per_chunk, per_chunk), per_chunk)

    def to_twin(part, turn, at_core):
        lanes = pl.ds(*LANES[part])
        half_at = pl.ds(pl.multiple_of((1 - at_core) * half, 16), half)
        return pltpu.make_async_remote_copy(
            src_ref=wb_v.at[chunk_at(turn), half_at, lanes],
            dst_ref=wa_v.at[chunk_at(turn), :, lanes],
            send_sem=a_send.at[part, turn],
            recv_sem=a_recv.at[part, turn],
            device_id=at_seq(twin),
            device_id_type=MESH,
        )

    def to_x(part, turn, step):
        lanes = pl.ds(*LANES[part])
        peer = lax.rem(xme + step, n_x)
        return pltpu.make_async_remote_copy(
            src_ref=wsb_v.at[peer, chunk_at(turn), :, lanes],
            dst_ref=wrb_v.at[step - 1, chunk_at(turn), :, lanes],
            send_sem=b_send.at[part, step - 1, turn],
            recv_sem=b_recv.at[part, step - 1, turn],
            device_id={"batch": peer},
            device_id_type=MESH,
        )

    if block > taps * chip_rows:
        pad = block - taps * chip_rows
        wb_v[:, pl.ds(taps * chip_rows, pad), :] = jnp.zeros((n_chip, pad, width), BF16)

    def weights(part):
        lane, many = LANES[part]
        lanes = pl.ds(lane, many)

        @pl.loop(0, CHUNKS)
        def _(turn):
            lhs = convt_v[pl.ds(pl.multiple_of(turn * chunk_rows, 16), chunk_rows), :]
            product = jnp.dot(
                lhs,
                wins_v[:, pl.ds(taps * lane, taps * many)],
                preferred_element_type=F32,
            )
            for place in range(per_chunk):
                for tap in range(taps):
                    wb_v[turn * per_chunk + place, pl.ds(tap * chip_rows, chip_rows), lanes] = (
                        product[
                            place * chip_rows : (place + 1) * chip_rows,
                            tap * many : (tap + 1) * many,
                        ].astype(BF16)
                    )
            to_twin(part, turn, core).start()

    def twin_sum(part):
        lanes = pl.ds(*LANES[part])

        @pl.loop(0, CHUNKS)
        def _(turn):
            to_twin(part, turn, core).wait_recv()
            at = chunk_at(turn)
            own_half = pl.multiple_of(core * half, 16)
            for q in range(n_x):
                total = wb_v[at, pl.ds(own_half + q * piece, piece), lanes].astype(F32) + wa_v[
                    at, pl.ds(q * piece, piece), lanes
                ].astype(F32)
                wsb_v[q, at, :, lanes] = total.astype(BF16)
            for step in range(1, n_x):
                to_x(part, turn, step).start()
            mine = pl.multiple_of(xme * piece, 16)
            wown_v[at, :, lanes] = wb_v[at, pl.ds(own_half + mine, piece), lanes].astype(
                F32
            ) + wa_v[at, pl.ds(mine, piece), lanes].astype(F32)

    pick = (
        lax.broadcasted_iota(jnp.int32, (TILE // 2, TILE), 1)
        == 2 * lax.broadcasted_iota(jnp.int32, (TILE // 2, TILE), 0)
    )
    pick = jnp.where(pick, 1.0, 0.0).astype(BF16)

    def outs(tile):
        at = pl.ds(pl.multiple_of(tile * TILE, TILE), TILE)
        low_at = pl.ds(pl.multiple_of(tile * (TILE // 2), TILE // 2), TILE // 2)
        return (
            pltpu.make_async_copy(skip_v.at[at], skip_ref.at[at], out_sem.at[tile]),
            pltpu.make_async_copy(
                lower_v.at[low_at], lower_ref.at[low_at], out_sem.at[share_tiles + tile]
            ),
        )

    def take_shares(part):
        lanes = pl.ds(*LANES[part])
        for index, begin, many in shares:
            share_to(part, index, begin, many).wait_recv()
            other_f[pl.ds(begin, many), lanes] = other_v[pl.ds(begin, many), lanes].astype(F32)

    def input_tile(part, tile):
        lane, many = LANES[part]
        lanes = pl.ds(lane, many)
        near = pl.multiple_of(BORDER - 8 + tile * TILE, 8)
        at = pl.ds(pl.multiple_of(tile * TILE, TILE), TILE)
        mine = slope_f[pl.ds(pl.multiple_of(ours + near, 8), TILE + 16), lanes]
        other = other_f[pl.ds(near, TILE + 16), lanes]
        for tap in range(taps):
            begin = 8 + reach - tap
            window = jnp.concatenate(
                [mine[begin : begin + TILE].astype(BF16), other[begin : begin + TILE].astype(BF16)],
                axis=1,
            )
            product = lax.dot_general(
                window,
                kfull_v[tap, :, pl.ds(2 * lane, 2 * many)],
                (((1,), (1,)), ((), ())),
                preferred_element_type=F32,
            )
            if part == 0 and tap == 0:
                acc_v[at, :] = product
            else:
                acc_v[at, :] += product
        if part == last_part:
            total = acc_v[at, :]
            paired = (total + pltpu.roll(total, TILE - 1, 0)).astype(BF16)
            low_at = pl.ds(pl.multiple_of(tile * (TILE // 2), TILE // 2), TILE // 2)
            skip_v[at, :] = total.astype(BF16)
            lower_v[low_at, :] = jnp.dot(pick, paired, preferred_element_type=F32).astype(BF16)
            for copy in outs(tile):
                copy.start()

    def to_chip(part, target, slot):
        lanes = pl.ds(*LANES[part])
        return pltpu.make_async_remote_copy(
            src_ref=wsc_v.at[target, :, lanes],
            dst_ref=wrc_v.at[slot, :, lanes],
            send_sem=c_send.at[part, slot],
            recv_sem=c_recv.at[part, slot],
            device_id=at_seq(2 * target + core),
            device_id_type=MESH,
        )

    def x_sum(part, turn):
        lanes = pl.ds(*LANES[part])
        at = chunk_at(turn)
        for step in range(1, n_x):
            to_x(part, turn, step).wait_recv()
        total = wown_v[at, :, lanes]
        for step in range(1, n_x):
            total = total + wrb_v[step - 1, at, :, lanes].astype(F32)
        wown_v[at, :, lanes] = total
        for i in range(per_chunk):
            target = turn + CHUNKS * i
            wsc_v[target, :, lanes] = total[i].astype(BF16)

            @pl.when(target != chip)
            def _():
                to_chip(part, target, lax.rem(target - chip + n_chip, n_chip)).start()

    junction(0, 0, 5)
    slopes_inner(0)
    junction(1, 0, 1)
    slopes_outer(0)
    weights(0)
    for way, part in halves:
        kernel_across(way, part, up).wait_recv()
        kernel_twin(way, part, core).start()
    twin_sum(0)
    junction(1, 1, 5)
    slopes_inner(1)
    slopes_outer(1)
    weights(1)
    twin_sum(1)

    @pl.loop(0, CHUNKS)
    def _(turn):
        x_sum(0, turn)

    for way, part in halves:
        kernel_twin(way, part, 1 - core).wait_recv()
    loads[4].wait()
    loads[5].wait()
    take_shares(0)

    @pl.loop(0, share_tiles)
    def _(tile):
        input_tile(0, tile)

    @pl.loop(1, n_seq)
    def _(step):
        offsets_to(step).wait_send()
        for part in range(len(LANES)):
            grads_to(part, step).wait_send()

    for way, part in halves:
        kernel_across(way, part, up).wait_send()
        kernel_twin(way, part, core).wait_send()

    @pl.loop(0, CHUNKS)
    def _(turn):
        x_sum(1, turn)

    take_shares(1)

    @pl.loop(0, share_tiles)
    def _(tile):
        input_tile(1, tile)

    own_place = lax.rem(chip, CHUNKS) * per_chunk + chip // CHUNKS
    final = wown_v[own_place]
    for slot in range(1, n_chip):
        for part in range(len(LANES)):
            to_chip(part, chip, slot).wait_recv()
        final = final + wrc_v[slot].astype(F32)
    worker = core * n_x + xme
    wfin_v[worker] = final * scale

    def to_worker(index, target):
        return pltpu.make_async_remote_copy(
            src_ref=wfin_v.at[worker],
            dst_ref=wfin_v.at[worker],
            send_sem=d_send.at[index],
            recv_sem=d_recv.at[index],
            device_id=target,
            device_id_type=MESH,
        )

    def from_worker(index, who):
        return pltpu.make_async_remote_copy(
            src_ref=wfin_v.at[worker],
            dst_ref=wfin_v.at[who],
            send_sem=d_send.at[index],
            recv_sem=d_recv.at[index],
            device_id=at_seq(twin),
            device_id_type=MESH,
        )

    for step in range(n_x):
        peer = lax.rem(xme + step, n_x)
        to_worker(step, {"seq": twin, "batch": peer}).start()
        if step:
            to_worker(n_x + step, {"batch": peer}).start()
    for step in range(n_x):
        peer = lax.rem(xme + n_x - step, n_x)
        from_worker(step, (1 - core) * n_x + peer).wait_recv()
        if step:
            from_worker(n_x + step, core * n_x + peer).wait_recv()

    whole = wfin_v[...].reshape(block, width)
    upper = jnp.concatenate(
        [
            whole[tap * chip_rows : tap * chip_rows + chip_rows // 2][None]
            for tap in range(taps)
        ]
    )
    under = jnp.concatenate(
        [
            whole[tap * chip_rows + chip_rows // 2 : (tap + 1) * chip_rows][None]
            for tap in range(taps)
        ]
    )
    weight_ref[...] = jnp.where(core == 0, upper, under)

    for tile in range(share_tiles):
        for copy in outs(tile):
            copy.wait()

    for part in range(len(LANES)):

        @pl.when(me > 0)
        def _():
            halo(part, 0, before).wait_send()

        @pl.when(me < n_seq - 1)
        def _():
            halo(part, 1, after).wait_send()

        for index, begin, many in shares:
            share_to(part, index, begin, many).wait_send()
        for turn in range(CHUNKS):
            to_twin(part, turn, core).wait_send()
            for step in range(1, n_x):
                to_x(part, turn, step).wait_send()
        for slot in range(1, n_chip):
            to_chip(part, chip, slot).wait_send()
    for step in range(n_x):
        to_worker(step, at_seq(twin)).wait_send()
        if step:
            to_worker(n_x + step, at_seq(twin)).wait_send()


def hand_over(skip_ref, lower_ref, weight_ref, skip_out, lower_out, weight_out):
    skip_out[...] = skip_ref[...]
    lower_out[...] = lower_ref[...]
    weight_out[...] = weight_ref[...]


def shards(
    conv_input, pre_activation, track_gradient, kernel, pair_rows, pair_count, pair_gradient
):
    n_seq, n_x = lax.axis_size("seq"), lax.axis_size("batch")
    rows_dev, width = track_gradient.shape[1:]
    depth = conv_input.shape[2]
    taps = kernel.shape[0]
    pairs = pair_rows.shape[1]
    endpoints = 2 * pairs
    cap = min(endpoints, 6 * pairs // n_seq)
    n_chip = n_seq // 2
    share = rows_dev // 2
    share_tiles = share // TILE
    chip_rows = depth // n_chip
    unit = 32 * n_x
    block = -(-taps * chip_rows // unit) * unit
    half = block // 2
    piece = half // n_x
    scale = (rows_dev * n_seq * n_x) ** -0.5
    sizes = (n_seq, n_x, cap, rows_dev, width, depth, taps, scale)
    any_spec = pl.BlockSpec(memory_space=pl.ANY)
    vmem = pltpu.VMEM
    dma = pltpu.SemaphoreType.DMA
    skip, lower, weight = pl.pallas_call(
        functools.partial(body, sizes),
        out_shape=(
            jax.ShapeDtypeStruct((share, depth), BF16),
            jax.ShapeDtypeStruct((share // 2, depth), BF16),
            jax.ShapeDtypeStruct((taps, chip_rows // 2, width), F32),
        ),
        in_specs=[
            pl.BlockSpec(memory_space=pltpu.VMEM),
            pl.BlockSpec(memory_space=pltpu.SMEM),
        ]
        + [any_spec] * 5,
        out_specs=(any_spec, any_spec, pl.BlockSpec(memory_space=pltpu.VMEM)),
        scratch_shapes=[
            vmem((pairs, 2, width), BF16),
            vmem((endpoints, width), BF16),
            vmem((n_seq, endpoints), jnp.int32),
            vmem((PACK * SLOT_ROWS, endpoints), BF16),
            vmem((n_seq, cap, width), BF16),
            vmem((n_seq * cap, width), BF16),
            vmem((n_seq, 1, SLOT_ROWS), F32),
            vmem((n_seq, 1, SLOT_ROWS), F32),
            vmem((rows_dev, width), BF16),
            vmem((rows_dev, width), BF16),
            vmem((rows_dev, depth), BF16),
            vmem((depth, rows_dev), BF16),
            vmem((rows_dev + 2 * BORDER, width), F32),
            vmem((rows_dev, width), F32),
            vmem((taps, depth, 2 * width), BF16),
            vmem((share + 2 * BORDER, width), BF16),
            vmem((share + 2 * BORDER, width), BF16),
            vmem((share + 2 * BORDER, width), F32),
            vmem((rows_dev, taps * width), BF16),
            vmem((share, depth), F32),
            vmem((n_chip, block, width), BF16),
            vmem((n_chip, half, width), BF16),
            vmem((n_x, n_chip, piece, width), BF16),
            vmem((n_x - 1, n_chip, piece, width), BF16),
            vmem((n_chip, piece, width), F32),
            vmem((n_chip, piece, width), BF16),
            vmem((n_chip, piece, width), BF16),
            vmem((2 * n_x, piece, width), F32),
            vmem((share, depth), BF16),
            vmem((share // 2, depth), BF16),
            dma((6,)),
            dma((2, n_seq)),
            dma((2, n_seq)),
            dma((n_seq,)),
            dma((n_seq,)),
            dma((2, 2)),
            dma((2, 2)),
            dma((2, 2)),
            dma((2, 2)),
            dma((2, 2)),
            dma((2, 2)),
            dma((2, share_tiles + 2)),
            dma((2, share_tiles + 2)),
            dma((2, CHUNKS)),
            dma((2, CHUNKS)),
            dma((2, n_x - 1, CHUNKS)),
            dma((2, n_x - 1, CHUNKS)),
            dma((2, n_chip)),
            dma((2, n_chip)),
            dma((2 * n_x,)),
            dma((2 * n_x,)),
            dma((2 * share_tiles,)),
        ],
        compiler_params=pltpu.CompilerParams(
            collective_id=0, has_side_effects=True, vmem_limit_bytes=63 * 1024 * 1024
        ),
    )(
        pair_rows[0].reshape(1, endpoints),
        pair_count,
        pair_gradient[0],
        track_gradient[0],
        pre_activation[0],
        conv_input[0],
        kernel,
    )
    steps = 4
    specs = (
        pl.BlockSpec((share // steps, depth), lambda i: (i, 0)),
        pl.BlockSpec((share // 2 // steps, depth), lambda i: (i, 0)),
        pl.BlockSpec((taps, chip_rows // 2, width), lambda i: (0, 0, 0)),
    )
    skip, lower, weight = pl.pallas_call(
        hand_over,
        grid=(steps,),
        out_shape=tuple(jax.ShapeDtypeStruct(a.shape, a.dtype) for a in (skip, lower, weight)),
        in_specs=specs,
        out_specs=specs,
    )(skip, lower, weight)
    return skip[None], lower[None], weight


def solution(mesh):
    in_specs = (
        P("batch", "seq", None),
        P("batch", "seq", "mp"),
        P("batch", "seq", "mp"),
        P(None, None, "mp"),
        P("batch", "seq", None),
        P("batch", "seq"),
        P("batch", "seq", None, "mp"),
    )
    out_specs = (
        P("batch", ("seq", "mp"), None),
        P("batch", ("seq", "mp"), None),
        P(None, "seq", "mp"),
    )
    return jax.shard_map(shards, mesh=mesh, in_specs=in_specs, out_specs=out_specs, check_vma=False)
```

```python
import functools

import jax
import jax.numpy as jnp
from jax import lax
from jax.experimental import pallas as pl
from jax.experimental.pallas import tpu as pltpu
from jax.sharding import PartitionSpec as P

MESH = pl.DeviceIdType.MESH
F32 = jnp.float32
BF16 = jnp.bfloat16
root_half = 0.7071067811865476
inv_root_tau = 0.3989422804014327
TILE = 256
BORDER = 16
CHUNKS = 4
PACK = 4
SLOT_ROWS = 128
LANES = ((0, 256), (256, 128))


def gelu_slope(values):
    normal_cdf = 0.5 * (1.0 + lax.erf(values * root_half))
    return normal_cdf + values * inv_root_tau * jnp.exp(-0.5 * values * values)


def body(
    sizes,
    rows_ref, count_ref, pairs_ref, track_ref, pre_ref, conv_ref, kern_ref,
    skip_ref, lower_ref, weight_ref,
    raw_v, pairs_v, slot_v, onehot_v, send_v, recv_v, soff_v, roff_v,
    track_v, pre_v, conv_v, convt_v, slope_f, grad_v, kfull_v,
    share_v, other_v, other_f, wins_v, acc_v,
    wb_v, wa_v, wsb_v, wrb_v, wown_v, wsc_v, wrc_v, wfin_v,
    skip_v, lower_v,
    load_sem, g_send, g_recv, o_send, o_recv, kx_send, kx_recv, kc_send, kc_recv,
    h_send, h_recv, m_send, m_recv, a_send, a_recv, b_send, b_recv,
    c_send, c_recv, d_send, d_recv, out_sem,
):
    n_seq, n_x, cap, rows_dev, width, depth, taps, scale = sizes
    n_chip = n_seq // 2
    n_z = n_chip // 2
    reach = taps // 2
    endpoints = 2 * pairs_ref.shape[0]
    share = rows_dev // 2
    tiles = rows_dev // TILE
    share_tiles = share // TILE
    chip_rows = depth // n_chip
    block = wb_v.shape[1]
    half = block // 2
    piece = half // n_x
    per_chunk = n_chip // CHUNKS
    chunk_rows = chip_rows * per_chunk
    quarter = depth // 4

    me = lax.axis_index("seq")
    mp = lax.axis_index("mp")
    xme = lax.axis_index("batch")
    core = lax.rem(me, 2)
    chip = me // 2
    yhi = chip // n_z
    zme = lax.rem(chip, n_z)
    twin = me + 1 - 2 * core

    def at_seq(target):
        return {"seq": target}

    up = {"seq": (lax.rem(yhi + mp, 2) * n_z + zme) * 2 + core, "mp": 1 - mp}
    down = {"seq": (lax.rem(yhi + 1 - mp, 2) * n_z + zme) * 2 + core, "mp": 1 - mp}

    loads = [
        pltpu.make_async_copy(pairs_ref, raw_v, load_sem.at[0]),
        pltpu.make_async_copy(pre_ref, pre_v, load_sem.at[1]),
        pltpu.make_async_copy(track_ref, track_v, load_sem.at[2]),
        pltpu.make_async_copy(conv_ref, conv_v, load_sem.at[3]),
    ] + [
        pltpu.make_async_copy(
            kern_ref.at[:, :, pl.ds(lane, many)],
            kfull_v.at[:, :, pl.ds(2 * lane, many)],
            load_sem.at[4 + part],
        )
        for part, (lane, many) in enumerate(LANES)
    ]
    for load in loads:
        load.start()

    barrier = pltpu.get_barrier_semaphore()

    def greet(target):
        pl.semaphore_signal(barrier, inc=1, device_id=target, device_id_type=MESH)

    @pl.loop(1, n_seq)
    def _(step):
        greet(at_seq(lax.rem(me + step, n_seq)))

    @pl.loop(1, n_x)
    def _(step):
        peer = lax.rem(xme + step, n_x)
        greet({"batch": peer})
        greet({"seq": twin, "batch": peer})

    greet(up)
    greet(down)

    lane = lax.broadcasted_iota(jnp.int32, (1, endpoints), 1)
    rows = rows_ref[...]
    owner = rows // rows_dev
    offset = rows - owner * rows_dev
    owner = jnp.where(lane // 2 < count_ref[0, 0], owner, n_seq)
    hit = owner == lax.broadcasted_iota(jnp.int32, (n_seq, endpoints), 0)
    rank = hit.astype(jnp.int32)
    wide_lane = lax.broadcasted_iota(jnp.int32, (n_seq, endpoints), 1)
    shift = 1
    while shift < endpoints:
        rank = rank + jnp.where(wide_lane >= shift, pltpu.roll(rank, shift, 1), 0)
        shift *= 2
    slot_v[...] = jnp.where(hit, rank - 1, -1)
    kind = lax.broadcasted_iota(jnp.int32, (16, endpoints), 0)
    parts = jnp.where(kind == 0, offset // 64, jnp.where(kind == 1, lax.rem(offset, 64), 1))
    parts = parts.astype(F32).astype(BF16)

    loads[0].wait()
    pairs_v[...] = raw_v[...].reshape(endpoints, width)
    pl.semaphore_wait(barrier, (n_seq - 1) + 2 * (n_x - 1) + 2)

    def grads_to(part, step):
        lanes = pl.ds(*LANES[part])
        return pltpu.make_async_remote_copy(
            src_ref=send_v.at[step, :, lanes],
            dst_ref=recv_v.at[pl.ds(pl.multiple_of(step * cap, 16), cap), lanes],
            send_sem=g_send.at[part, step],
            recv_sem=g_recv.at[part, step],
            device_id=at_seq(lax.rem(me + step, n_seq)),
            device_id_type=MESH,
        )

    def offsets_to(step):
        return pltpu.make_async_remote_copy(
            src_ref=soff_v.at[step],
            dst_ref=roff_v.at[step],
            send_sem=o_send.at[step],
            recv_sem=o_recv.at[step],
            device_id=at_seq(lax.rem(me + step, n_seq)),
            device_id_type=MESH,
        )

    def pack(first):
        for i in range(PACK):
            target = lax.rem(me + first + i, n_seq)
            slots = slot_v[pl.ds(target, 1), :].astype(F32).astype(BF16)
            places = lax.broadcasted_iota(jnp.int32, (SLOT_ROWS, endpoints), 0)
            onehot_v[pl.ds(i * SLOT_ROWS, SLOT_ROWS), :] = jnp.where(
                slots == places.astype(F32).astype(BF16), jnp.ones((), BF16), jnp.zeros((), BF16)
            )
        onehot = onehot_v[...]
        listed = jnp.dot(onehot, pairs_v[...], preferred_element_type=F32).astype(BF16)
        marks = lax.dot_general(
            parts, onehot, (((1,), (1,)), ((), ())), preferred_element_type=F32
        )
        where_to = jnp.where(marks[2:3] > 0.5, marks[0:1] * 64.0 + marks[1:2], -1.0)
        return listed, where_to

    def emit(first, begin):
        listed, where_to = pack(first)
        for i in range(PACK):
            some = listed[i * SLOT_ROWS : i * SLOT_ROWS + cap]
            place = where_to[:, i * SLOT_ROWS : (i + 1) * SLOT_ROWS]
            if i < begin:
                recv_v[pl.ds(0, cap), :] = some
                roff_v[0] = place
            else:
                send_v[first + i] = some
                soff_v[first + i] = place
                offsets_to(first + i).start()
                grads_to(0, first + i).start()

    def kernel_piece(index):
        return pl.ds(pl.multiple_of(index * quarter, 16), quarter)

    def kernel_across(way, part, target):
        lane, many = LANES[part]
        rows_at = kernel_piece(2 * core + way)
        return pltpu.make_async_remote_copy(
            src_ref=kern_ref.at[:, rows_at, pl.ds(lane, many)],
            dst_ref=kfull_v.at[:, rows_at, pl.ds(2 * lane + many, many)],
            send_sem=kx_send.at[way, part],
            recv_sem=kx_recv.at[way, part],
            device_id=target,
            device_id_type=MESH,
        )

    def kernel_twin(way, part, at_core):
        lane, many = LANES[part]
        region = kfull_v.at[:, kernel_piece(2 * at_core + way), pl.ds(2 * lane + many, many)]
        return pltpu.make_async_remote_copy(
            src_ref=region,
            dst_ref=region,
            send_sem=kc_send.at[way, part],
            recv_sem=kc_recv.at[way, part],
            device_id=at_seq(twin),
            device_id_type=MESH,
        )

    halves = [(way, part) for part in range(len(LANES)) for way in range(2)]
    for way, part in halves:
        kernel_across(way, part, down if way else up).start()

    emit(0, 1)

    @pl.loop(1, n_seq // PACK)
    def _(turn):
        emit(turn * PACK, 0)

    for part in range(1, len(LANES)):

        @pl.loop(1, n_seq)
        def _(step):
            grads_to(part, step).start()

    loads[1].wait()
    loads[2].wait()

    @pl.loop(0, tiles)
    def _(tile):
        at = pl.ds(pl.multiple_of(tile * TILE, TILE), TILE)
        grad_v[at, :] = gelu_slope(pre_v[at, :].astype(F32))
        slope_f[pl.ds(pl.multiple_of(BORDER + tile * TILE, BORDER), TILE), :] = track_v[
            at, :
        ].astype(F32)

    loads[3].wait()

    @pl.loop(0, tiles)
    def _(tile):
        at = pl.ds(pl.multiple_of(tile * TILE, TILE), TILE)
        turned = conv_v[at, :].T
        for place in range(n_chip):
            source = place // per_chunk + CHUNKS * (place % per_chunk)
            convt_v[pl.ds(place * chip_rows, chip_rows), at] = turned[
                source * chip_rows : (source + 1) * chip_rows
            ]

    tile_lane = lax.broadcasted_iota(jnp.int32, (1, SLOT_ROWS), 1)

    def four_lists(first):
        p = [roff_v[first + i] for i in range(4)]
        one = pltpu.roll(p[1], 96, 1)
        two = pltpu.roll(p[2], 64, 1)
        three = pltpu.roll(p[3], 32, 1)
        return jnp.concatenate(
            [
                jnp.where(tile_lane < 96, p[0], one),
                jnp.where(tile_lane < 64, one, two),
                jnp.where(tile_lane < 32, two, three),
            ],
            axis=1,
        )

    groups = [(first, 8) for first in range(0, n_seq - 8, 8)] + [(n_seq - 8, 4), (n_seq - 4, 4)]
    before = lax.rem(me + n_seq - 1, n_seq)
    after = lax.rem(me + 1, n_seq)
    low = pl.ds(BORDER - 8, 8)
    high = pl.ds(BORDER + rows_dev, 8)
    theirs = (1 - mp) * share
    ours = mp * share
    last_part = len(LANES) - 1

    few_rows = lax.broadcasted_iota(jnp.int32, (16, 8 * cap), 0).astype(F32).astype(BF16)
    one, zero = jnp.ones((), BF16), jnp.zeros((), BF16)

    def junction(part, begin_group, end_group):
        lanes = pl.ds(*LANES[part])
        for first, many in groups[begin_group:end_group]:
            @pl.loop(max(first, 1), first + many)
            def _(step):
                if part == 0:
                    offsets_to(step).wait_recv()
                grads_to(part, step).wait_recv()

            lists = jnp.concatenate([four_lists(first + i) for i in range(0, many, 4)], axis=1)
            ends = first + many == n_seq

            @pl.loop(0, tiles, unroll=8)
            def _(tile, first=first, many=many, lists=lists, ends=ends):
                wanted = (lists - (tile * TILE).astype(F32)).astype(BF16)
                wanted = jnp.broadcast_to(wanted, (16, many * cap))
                onehot = jnp.concatenate(
                    [
                        jnp.where(wanted == few_rows[:, : many * cap] + 16.0 * i, one, zero)
                        for i in range(TILE // 16)
                    ]
                )
                at = pl.ds(pl.multiple_of(BORDER + tile * TILE, BORDER), TILE)
                total = slope_f[at, lanes] + jnp.dot(
                    onehot,
                    recv_v[pl.ds(first * cap, many * cap), lanes],
                    preferred_element_type=F32,
                )
                if ends:
                    slope = grad_v[pl.ds(pl.multiple_of(tile * TILE, TILE), TILE), lanes]
                    total = (total * slope).astype(BF16).astype(F32)
                slope_f[at, lanes] = total

    def halo(part, way, target):
        lanes = pl.ds(*LANES[part])
        own = pl.ds(BORDER, 8) if way == 0 else pl.ds(BORDER + rows_dev - 8, 8)
        return pltpu.make_async_remote_copy(
            src_ref=slope_f.at[own, lanes],
            dst_ref=slope_f.at[high if way == 0 else low, lanes],
            send_sem=h_send.at[part, way],
            recv_sem=h_recv.at[part, way],
            device_id=at_seq(target),
            device_id_type=MESH,
        )

    def share_to(part, index, begin, many):
        lanes = pl.ds(*LANES[part])
        return pltpu.make_async_remote_copy(
            src_ref=share_v.at[pl.ds(begin, many), lanes],
            dst_ref=other_v.at[pl.ds(begin, many), lanes],
            send_sem=m_send.at[part, index],
            recv_sem=m_recv.at[part, index],
            device_id={"mp": 1 - mp},
            device_id_type=MESH,
        )

    shares = [(t, BORDER + t * TILE, TILE) for t in range(share_tiles)] + [
        (share_tiles, 0, BORDER),
        (share_tiles + 1, BORDER + share, BORDER),
    ]

    def send_share(part, index, begin, many):
        lanes = pl.ds(*LANES[part])
        share_v[pl.ds(begin, many), lanes] = slope_f[
            pl.ds(pl.multiple_of(theirs + begin, BORDER), many), lanes
        ].astype(BF16)
        share_to(part, index, begin, many).start()

    def windows(part, tile):
        lane, many = LANES[part]
        at = pl.ds(pl.multiple_of(tile * TILE, TILE), TILE)
        near = slope_f[
            pl.ds(pl.multiple_of(BORDER - 8 + tile * TILE, 8), TILE + 16), pl.ds(lane, many)
        ]
        for tap in range(taps):
            begin = 8 + reach - tap
            wins_v[at, pl.ds(taps * lane + tap * many, many)] = near[
                begin : begin + TILE
            ].astype(BF16)

    def slopes_inner(part):
        @pl.when(me > 0)
        def _():
            halo(part, 0, before).start()

        @pl.when(me < n_seq - 1)
        def _():
            halo(part, 1, after).start()

        for index, begin, rows_many in shares[:share_tiles]:
            send_share(part, index, begin, rows_many)

        @pl.loop(1, tiles - 1)
        def _(tile):
            windows(part, tile)

    def slopes_outer(part):
        lanes = pl.ds(*LANES[part])
        many = LANES[part][1]

        @pl.when(me < n_seq - 1)
        def _():
            halo(part, 0, before).wait_recv()

        @pl.when(me == n_seq - 1)
        def _():
            slope_f[high, lanes] = jnp.zeros((8, many), F32)

        @pl.when(me > 0)
        def _():
            halo(part, 1, after).wait_recv()

        @pl.when(me == 0)
        def _():
            slope_f[low, lanes] = jnp.zeros((8, many), F32)

        for index, begin, rows_many in shares[share_tiles:]:
            send_share(part, index, begin, rows_many)
        windows(part, 0)
        windows(part, tiles - 1)

    def chunk_at(turn):
        return pl.ds(pl.multiple_of(turn * per_chunk, per_chunk), per_chunk)

    def to_twin(part, turn, at_core):
        lanes = pl.ds(*LANES[part])
        half_at = pl.ds(pl.multiple_of((1 - at_core) * half, 16), half)
        return pltpu.make_async_remote_copy(
            src_ref=wb_v.at[chunk_at(turn), half_at, lanes],
            dst_ref=wa_v.at[chunk_at(turn), :, lanes],
            send_sem=a_send.at[part, turn],
            recv_sem=a_recv.at[part, turn],
            device_id=at_seq(twin),
            device_id_type=MESH,
        )

    def to_x(part, turn, step):
        lanes = pl.ds(*LANES[part])
        peer = lax.rem(xme + step, n_x)
        return pltpu.make_async_remote_copy(
            src_ref=wsb_v.at[peer, chunk_at(turn), :, lanes],
            dst_ref=wrb_v.at[step - 1, chunk_at(turn), :, lanes],
            send_sem=b_send.at[part, step - 1, turn],
            recv_sem=b_recv.at[part, step - 1, turn],
            device_id={"batch": peer},
            device_id_type=MESH,
        )

    if block > taps * chip_rows:
        pad = block - taps * chip_rows
        wb_v[:, pl.ds(taps * chip_rows, pad), :] = jnp.zeros((n_chip, pad, width), BF16)

    def weights(part):
        lane, many = LANES[part]
        lanes = pl.ds(lane, many)

        @pl.loop(0, CHUNKS)
        def _(turn):
            lhs = convt_v[pl.ds(pl.multiple_of(turn * chunk_rows, 16), chunk_rows), :]
            product = jnp.dot(
                lhs,
                wins_v[:, pl.ds(taps * lane, taps * many)],
                preferred_element_type=F32,
            )
            for place in range(per_chunk):
                for tap in range(taps):
                    wb_v[turn * per_chunk + place, pl.ds(tap * chip_rows, chip_rows), lanes] = (
                        product[
                            place * chip_rows : (place + 1) * chip_rows,
                            tap * many : (tap + 1) * many,
                        ].astype(BF16)
                    )
            to_twin(part, turn, core).start()

    def twin_sum(part):
        lanes = pl.ds(*LANES[part])

        @pl.loop(0, CHUNKS)
        def _(turn):
            to_twin(part, turn, core).wait_recv()
            at = chunk_at(turn)
            own_half = pl.multiple_of(core * half, 16)
            for q in range(n_x):
                total = wb_v[at, pl.ds(own_half + q * piece, piece), lanes].astype(F32) + wa_v[
                    at, pl.ds(q * piece, piece), lanes
                ].astype(F32)
                wsb_v[q, at, :, lanes] = total.astype(BF16)
            for step in range(1, n_x):
                to_x(part, turn, step).start()
            mine = pl.multiple_of(xme * piece, 16)
            wown_v[at, :, lanes] = wb_v[at, pl.ds(own_half + mine, piece), lanes].astype(
                F32
            ) + wa_v[at, pl.ds(mine, piece), lanes].astype(F32)

    pick = (
        lax.broadcasted_iota(jnp.int32, (TILE // 2, TILE), 1)
        == 2 * lax.broadcasted_iota(jnp.int32, (TILE // 2, TILE), 0)
    )
    pick = jnp.where(pick, 1.0, 0.0).astype(BF16)

    def outs(tile):
        at = pl.ds(pl.multiple_of(tile * TILE, TILE), TILE)
        low_at = pl.ds(pl.multiple_of(tile * (TILE // 2), TILE // 2), TILE // 2)
        return (
            pltpu.make_async_copy(skip_v.at[at], skip_ref.at[at], out_sem.at[tile]),
            pltpu.make_async_copy(
                lower_v.at[low_at], lower_ref.at[low_at], out_sem.at[share_tiles + tile]
            ),
        )

    def take_shares(part):
        lanes = pl.ds(*LANES[part])
        for index, begin, many in shares:
            share_to(part, index, begin, many).wait_recv()
            other_f[pl.ds(begin, many), lanes] = other_v[pl.ds(begin, many), lanes].astype(F32)

    def input_tile(part, tile):
        lane, many = LANES[part]
        lanes = pl.ds(lane, many)
        near = pl.multiple_of(BORDER - 8 + tile * TILE, 8)
        at = pl.ds(pl.multiple_of(tile * TILE, TILE), TILE)
        mine = slope_f[pl.ds(pl.multiple_of(ours + near, 8), TILE + 16), lanes]
        other = other_f[pl.ds(near, TILE + 16), lanes]
        for tap in range(taps):
            begin = 8 + reach - tap
            window = jnp.concatenate(
                [mine[begin : begin + TILE].astype(BF16), other[begin : begin + TILE].astype(BF16)],
                axis=1,
            )
            product = lax.dot_general(
                window,
                kfull_v[tap, :, pl.ds(2 * lane, 2 * many)],
                (((1,), (1,)), ((), ())),
                preferred_element_type=F32,
            )
            if part == 0 and tap == 0:
                acc_v[at, :] = product
            else:
                acc_v[at, :] += product
        if part == last_part:
            total = acc_v[at, :]
            paired = (total + pltpu.roll(total, TILE - 1, 0)).astype(BF16)
            low_at = pl.ds(pl.multiple_of(tile * (TILE // 2), TILE // 2), TILE // 2)
            skip_v[at, :] = total.astype(BF16)
            lower_v[low_at, :] = jnp.dot(pick, paired, preferred_element_type=F32).astype(BF16)
            for copy in outs(tile):
                copy.start()

    def to_chip(part, target, slot):
        lanes = pl.ds(*LANES[part])
        return pltpu.make_async_remote_copy(
            src_ref=wsc_v.at[target, :, lanes],
            dst_ref=wrc_v.at[slot, :, lanes],
            send_sem=c_send.at[part, slot],
            recv_sem=c_recv.at[part, slot],
            device_id=at_seq(2 * target + core),
            device_id_type=MESH,
        )

    def x_sum(part, turn):
        lanes = pl.ds(*LANES[part])
        at = chunk_at(turn)
        for step in range(1, n_x):
            to_x(part, turn, step).wait_recv()
        total = wown_v[at, :, lanes]
        for step in range(1, n_x):
            total = total + wrb_v[step - 1, at, :, lanes].astype(F32)
        wown_v[at, :, lanes] = total
        for i in range(per_chunk):
            target = turn + CHUNKS * i
            wsc_v[target, :, lanes] = total[i].astype(BF16)

            @pl.when(target != chip)
            def _():
                to_chip(part, target, lax.rem(target - chip + n_chip, n_chip)).start()

    junction(0, 0, 5)
    slopes_inner(0)
    junction(1, 0, 1)
    slopes_outer(0)
    weights(0)
    for way, part in halves:
        kernel_across(way, part, up).wait_recv()
        kernel_twin(way, part, core).start()
    twin_sum(0)
    junction(1, 1, 5)
    slopes_inner(1)
    slopes_outer(1)
    weights(1)
    twin_sum(1)

    @pl.loop(0, CHUNKS)
    def _(turn):
        x_sum(0, turn)

    for way, part in halves:
        kernel_twin(way, part, 1 - core).wait_recv()
    loads[4].wait()
    loads[5].wait()
    take_shares(0)

    @pl.loop(0, share_tiles)
    def _(tile):
        input_tile(0, tile)

    @pl.loop(1, n_seq)
    def _(step):
        offsets_to(step).wait_send()
        for part in range(len(LANES)):
            grads_to(part, step).wait_send()

    for way, part in halves:
        kernel_across(way, part, up).wait_send()
        kernel_twin(way, part, core).wait_send()

    @pl.loop(0, CHUNKS)
    def _(turn):
        x_sum(1, turn)

    take_shares(1)

    @pl.loop(0, share_tiles)
    def _(tile):
        input_tile(1, tile)

    own_place = lax.rem(chip, CHUNKS) * per_chunk + chip // CHUNKS
    final = wown_v[own_place]
    for slot in range(1, n_chip):
        for part in range(len(LANES)):
            to_chip(part, chip, slot).wait_recv()
        final = final + wrc_v[slot].astype(F32)
    worker = core * n_x + xme
    wfin_v[worker] = final * scale

    def to_worker(index, target):
        return pltpu.make_async_remote_copy(
            src_ref=wfin_v.at[worker],
            dst_ref=wfin_v.at[worker],
            send_sem=d_send.at[index],
            recv_sem=d_recv.at[index],
            device_id=target,
            device_id_type=MESH,
        )

    def from_worker(index, who):
        return pltpu.make_async_remote_copy(
            src_ref=wfin_v.at[worker],
            dst_ref=wfin_v.at[who],
            send_sem=d_send.at[index],
            recv_sem=d_recv.at[index],
            device_id=at_seq(twin),
            device_id_type=MESH,
        )

    for step in range(n_x):
        peer = lax.rem(xme + step, n_x)
        to_worker(step, {"seq": twin, "batch": peer}).start()
        if step:
            to_worker(n_x + step, {"batch": peer}).start()
    for step in range(n_x):
        peer = lax.rem(xme + n_x - step, n_x)
        from_worker(step, (1 - core) * n_x + peer).wait_recv()
        if step:
            from_worker(n_x + step, core * n_x + peer).wait_recv()

    whole = wfin_v[...].reshape(block, width)
    upper = jnp.concatenate(
        [
            whole[tap * chip_rows : tap * chip_rows + chip_rows // 2][None]
            for tap in range(taps)
        ]
    )
    under = jnp.concatenate(
        [
            whole[tap * chip_rows + chip_rows // 2 : (tap + 1) * chip_rows][None]
            for tap in range(taps)
        ]
    )
    weight_ref[...] = jnp.where(core == 0, upper, under)

    for tile in range(share_tiles):
        for copy in outs(tile):
            copy.wait()

    for part in range(len(LANES)):

        @pl.when(me > 0)
        def _():
            halo(part, 0, before).wait_send()

        @pl.when(me < n_seq - 1)
        def _():
            halo(part, 1, after).wait_send()

        for index, begin, many in shares:
            share_to(part, index, begin, many).wait_send()
        for turn in range(CHUNKS):
            to_twin(part, turn, core).wait_send()
            for step in range(1, n_x):
                to_x(part, turn, step).wait_send()
        for slot in range(1, n_chip):
            to_chip(part, chip, slot).wait_send()
    for step in range(n_x):
        to_worker(step, at_seq(twin)).wait_send()
        if step:
            to_worker(n_x + step, at_seq(twin)).wait_send()


def hand_over(skip_ref, lower_ref, weight_ref, skip_out, lower_out, weight_out):
    skip_out[...] = skip_ref[...]
    lower_out[...] = lower_ref[...]
    weight_out[...] = weight_ref[...]


def shards(
    conv_input, pre_activation, track_gradient, kernel, pair_rows, pair_count, pair_gradient
):
    n_seq, n_x = lax.axis_size("seq"), lax.axis_size("batch")
    rows_dev, width = track_gradient.shape[1:]
    depth = conv_input.shape[2]
    taps = kernel.shape[0]
    pairs = pair_rows.shape[1]
    endpoints = 2 * pairs
    cap = min(endpoints, 6 * pairs // n_seq)
    n_chip = n_seq // 2
    share = rows_dev // 2
    share_tiles = share // TILE
    chip_rows = depth // n_chip
    unit = 32 * n_x
    block = -(-taps * chip_rows // unit) * unit
    half = block // 2
    piece = half // n_x
    scale = (rows_dev * n_seq * n_x) ** -0.5
    sizes = (n_seq, n_x, cap, rows_dev, width, depth, taps, scale)
    any_spec = pl.BlockSpec(memory_space=pl.ANY)
    vmem = pltpu.VMEM
    dma = pltpu.SemaphoreType.DMA
    skip, lower, weight = pl.pallas_call(
        functools.partial(body, sizes),
        out_shape=(
            jax.ShapeDtypeStruct((share, depth), BF16),
            jax.ShapeDtypeStruct((share // 2, depth), BF16),
            jax.ShapeDtypeStruct((taps, chip_rows // 2, width), F32),
        ),
        in_specs=[
            pl.BlockSpec(memory_space=pltpu.VMEM),
            pl.BlockSpec(memory_space=pltpu.SMEM),
        ]
        + [any_spec] * 5,
        out_specs=(any_spec, any_spec, pl.BlockSpec(memory_space=pltpu.VMEM)),
        scratch_shapes=[
            vmem((pairs, 2, width), BF16),
            vmem((endpoints, width), BF16),
            vmem((n_seq, endpoints), jnp.int32),
            vmem((PACK * SLOT_ROWS, endpoints), BF16),
            vmem((n_seq, cap, width), BF16),
            vmem((n_seq * cap, width), BF16),
            vmem((n_seq, 1, SLOT_ROWS), F32),
            vmem((n_seq, 1, SLOT_ROWS), F32),
            vmem((rows_dev, width), BF16),
            vmem((rows_dev, width), BF16),
            vmem((rows_dev, depth), BF16),
            vmem((depth, rows_dev), BF16),
            vmem((rows_dev + 2 * BORDER, width), F32),
            vmem((rows_dev, width), F32),
            vmem((taps, depth, 2 * width), BF16),
            vmem((share + 2 * BORDER, width), BF16),
            vmem((share + 2 * BORDER, width), BF16),
            vmem((share + 2 * BORDER, width), F32),
            vmem((rows_dev, taps * width), BF16),
            vmem((share, depth), F32),
            vmem((n_chip, block, width), BF16),
            vmem((n_chip, half, width), BF16),
            vmem((n_x, n_chip, piece, width), BF16),
            vmem((n_x - 1, n_chip, piece, width), BF16),
            vmem((n_chip, piece, width), F32),
            vmem((n_chip, piece, width), BF16),
            vmem((n_chip, piece, width), BF16),
            vmem((2 * n_x, piece, width), F32),
            vmem((share, depth), BF16),
            vmem((share // 2, depth), BF16),
            dma((6,)),
            dma((2, n_seq)),
            dma((2, n_seq)),
            dma((n_seq,)),
            dma((n_seq,)),
            dma((2, 2)),
            dma((2, 2)),
            dma((2, 2)),
            dma((2, 2)),
            dma((2, 2)),
            dma((2, 2)),
            dma((2, share_tiles + 2)),
            dma((2, share_tiles + 2)),
            dma((2, CHUNKS)),
            dma((2, CHUNKS)),
            dma((2, n_x - 1, CHUNKS)),
            dma((2, n_x - 1, CHUNKS)),
            dma((2, n_chip)),
            dma((2, n_chip)),
            dma((2 * n_x,)),
            dma((2 * n_x,)),
            dma((2 * share_tiles,)),
        ],
        compiler_params=pltpu.CompilerParams(
            collective_id=0, has_side_effects=True, vmem_limit_bytes=63 * 1024 * 1024
        ),
    )(
        pair_rows[0].reshape(1, endpoints),
        pair_count,
        pair_gradient[0],
        track_gradient[0],
        pre_activation[0],
        conv_input[0],
        kernel,
    )
    steps = 4
    specs = (
        pl.BlockSpec((share // steps, depth), lambda i: (i, 0)),
        pl.BlockSpec((share // 2 // steps, depth), lambda i: (i, 0)),
        pl.BlockSpec((taps, chip_rows // 2, width), lambda i: (0, 0, 0)),
    )
    skip, lower, weight = pl.pallas_call(
        hand_over,
        grid=(steps,),
        out_shape=tuple(jax.ShapeDtypeStruct(a.shape, a.dtype) for a in (skip, lower, weight)),
        in_specs=specs,
        out_specs=specs,
    )(skip, lower, weight)
    return skip[None], lower[None], weight


def solution(mesh):
    in_specs = (
        P("batch", "seq", None),
        P("batch", "seq", "mp"),
        P("batch", "seq", "mp"),
        P(None, None, "mp"),
        P("batch", "seq", None),
        P("batch", "seq"),
        P("batch", "seq", None, "mp"),
    )
    out_specs = (
        P("batch", ("seq", "mp"), None),
        P("batch", ("seq", "mp"), None),
        P(None, "seq", "mp"),
    )
    return jax.shard_map(shards, mesh=mesh, in_specs=in_specs, out_specs=out_specs, check_vma=False)
```
